512 devices in a mesh: dp: 32 (over x, y, core), mp: 16 (over z).
Axes of the slice: x: 4, y: 4, z: 16, core: 2. Of those that a mesh axis runs over, the one named last changes fastest.
Arguments:
- grads: bfloat16 [32, 1024, 10240], P('dp', None, 'mp'), may hold values from -4 to 4
- left_factor: float32 [16, 3, 1024, 1024], P('mp', None, 'dp'), may hold values from -0.3 to 0.3
- left_root: bfloat16 [16, 3, 1024, 1024], P('mp', None, 'dp'), may hold values from -2.5 to 2.5
- right_q: float32 [16, 512, 512], P('mp', 'dp'), may hold values from -0.3 to 0.3
- right_kv: float32 [16, 2, 64, 64], P('mp'), may hold values from -0.3 to 0.3
- right_q_root: bfloat16 [16, 512, 512], P('mp'), may hold values from -2.5 to 2.5
- right_kv_root: bfloat16 [16, 2, 64, 64], P('mp'), may hold values from -2.5 to 2.5
- moment: float32 [1024, 10240], P('dp', 'mp'), may hold values from 0.001 to 0.1
Outputs:
- direction: bfloat16 [1024, 10240], P(None, 'mp')
- left_new: float32 [16, 3, 1024, 1024], P('mp', None, 'dp')
- right_q_new: float32 [16, 512, 512], P('mp', 'dp')
- right_kv_new: float32 [16, 2, 64, 64], P('mp')
- moment_new: float32 [1024, 10240], P('dp', 'mp')
The draws below stay inside these ranges and needn't reach their ends.
All inputs are finite; a program needn't handle non-finite values.
Results may differ from the reference program's by a relative error of at most 0.024.
Values may be sent and summed in bfloat16 or wider, within the bound.
A program may use at most 64 MiB of HBM per device.

```python
import math
import jax
import jax.numpy as jnp
from jax import lax

B = 1024
CQ = 512
CKV = 64
C_ALL = 10240
N_DP = 32
N_MP = 16


def sample_roots(key, leading, order):
    diag_key, noise_key = jax.random.split(key)
    diagonal = jnp.exp(jax.random.uniform(diag_key, leading + (order, 1), jnp.float32, math.log(0.5), math.log(2.0)))
    noise = jnp.clip(jax.random.normal(noise_key, leading + (order, order), jnp.float32), -6.0, 6.0) * (0.5 / math.sqrt(order))
    identity = (jnp.arange(order)[:, None] == jnp.arange(order)[None, :]).astype(jnp.float32)
    return jnp.clip(diagonal * identity + noise, -2.5, 2.5)


def draw_grads(key, part):
    key = jax.random.fold_in(key, 1)
    noise_key, row_key, col_key = jax.random.split(key, 3)
    row_ramp = 1.0 + 2.0 * jnp.arange(B, dtype=jnp.float32) / (B - 1)
    col_ramp = 1.0 + 2.0 * jnp.arange(C_ALL, dtype=jnp.float32) / (C_ALL - 1)
    row_scale = row_ramp * jnp.exp(jax.random.uniform(row_key, (B,), jnp.float32, 0.0, math.log(3.0)))
    col_scale = col_ramp * jnp.exp(jax.random.uniform(col_key, (C_ALL,), jnp.float32, 0.0, math.log(3.0)))
    noise = jnp.clip(jax.random.normal(noise_key, (N_DP, B, C_ALL), jnp.float32), -6.0, 6.0)
    values = 0.01 * noise / math.sqrt(N_DP)
    values = values * row_scale[None, :, None] * col_scale[None, None, :]
    return jnp.clip(values, -4.0, 4.0).astype(jnp.bfloat16)


def draw_left_root(key, part):
    key = jax.random.fold_in(key, 2)
    return sample_roots(key, (N_MP, 3), B).astype(jnp.bfloat16)


def draw_right_q_root(key, part):
    key = jax.random.fold_in(key, 3)
    return sample_roots(key, (N_MP,), CQ).astype(jnp.bfloat16)


def draw_right_kv_root(key, part):
    key = jax.random.fold_in(key, 4)
    return sample_roots(key, (N_MP, 2), CKV).astype(jnp.bfloat16)


def shard_levels(stream_key, shape, cuts, smallest, top_value):
    def one(dim, parts):
        draws = jax.random.uniform(jax.random.fold_in(jax.random.fold_in(stream_key, 6), dim), (parts,), jnp.float32, smallest / len(cuts), top_value / len(cuts))
        return jnp.repeat(jnp.exp(draws), shape[dim] // parts).reshape((-1,) + (1,) * (len(shape) - dim - 1))

    loudness = one(*cuts[0])
    for cut in cuts[1:]:
        loudness = loudness * one(*cut)
    return loudness


def normal_values(own_key, dims, deviation, most, cuts=(), held_as=jnp.bfloat16):
    level = shard_levels(own_key, dims, cuts, -0.22, 0.18) if cuts else 1.0
    entries = jax.random.normal(own_key, dims, jnp.float32) * deviation * level
    return jnp.minimum(jnp.maximum(entries, -most), most).astype(held_as)


def setup_inputs(seed: int = 0) -> dict:
    streams_of = jax.random.split(jax.random.key(seed), 9)
    return {
        "grads": draw_grads(jax.random.fold_in(streams_of[8], 71), 0),
        "left_factor": normal_values(streams_of[1], (N_MP, 3, B, B), 0.05, 0.3, ((0, 16), (2, 32)), jnp.float32),
        "left_root": draw_left_root(jax.random.fold_in(streams_of[8], 71), 0),
        "right_q": normal_values(streams_of[3], (N_MP, CQ, CQ), 0.05, 0.3, ((0, 16), (1, 32)), jnp.float32),
        "right_kv": normal_values(streams_of[4], (N_MP, 2, CKV, CKV), 0.05, 0.3, ((0, 16),), jnp.float32),
        "right_q_root": draw_right_q_root(jax.random.fold_in(streams_of[8], 71), 0),
        "right_kv_root": draw_right_kv_root(jax.random.fold_in(streams_of[8], 71), 0),
        "moment": jnp.clip(jnp.exp(math.log(0.1) - 4.6051702 * jax.random.uniform(streams_of[7], (B, C_ALL), jnp.float32) ** shard_levels(streams_of[7], (B, C_ALL), ((0, 32), (1, 16)), -0.2, 0.2)), 0.001, 0.1),
    }


factor_keep = 0.95
factor_add = 0.05
moment_keep = 0.99
moment_add = 0.01
graft_eps = 1e-08
norm_eps = 1e-06

def block_spans(q_cols, kv_cols):
    return ((0, q_cols), (q_cols, kv_cols), (q_cols + kv_cols, kv_cols))

def row_product(first, second):
    return lax.dot_general(first, second, (((1,), (1,)), ((), ())), preferred_element_type=jnp.float32)

def column_product(first, second):
    return lax.dot_general(first, second, (((0,), (0,)), ((), ())), preferred_element_type=jnp.float32)

def reference(grads, left_factor, left_root, right_q, right_kv, right_q_root, right_kv_root, moment):
    total = lax.optimization_barrier(jnp.sum(grads.astype(jnp.float32), axis=0)).astype(jnp.bfloat16)
    shard_cols = CQ + 2 * CKV
    spans = block_spans(CQ, CKV)
    widened = total.astype(jnp.float32)
    moment_new = moment_keep * moment + moment_add * widened * widened
    graft = widened / (jnp.sqrt(moment_new) + graft_eps)
    left_all = []
    right_q_all = []
    right_kv_all = []
    precond_all = []
    for shard in range(N_MP):
        slab = total[:, shard * shard_cols:(shard + 1) * shard_cols]
        lefts = []
        conds = []
        kv_list = []
        for number in range(3):
            offset, extent = spans[number]
            block_grad = slab[:, offset:offset + extent]
            lefts.append(factor_keep * left_factor[shard, number] + factor_add * row_product(block_grad, block_grad))
            projected = jnp.dot(left_root[shard, number], block_grad, preferred_element_type=jnp.float32).astype(jnp.bfloat16)
            if number == 0:
                root_block = right_q_root[shard]
                right_q_all.append(factor_keep * right_q[shard] + factor_add * column_product(block_grad, block_grad))
            else:
                root_block = right_kv_root[shard, number - 1]
                kv_list.append(factor_keep * right_kv[shard, number - 1] + factor_add * column_product(block_grad, block_grad))
            conds.append(jnp.dot(projected, root_block, preferred_element_type=jnp.float32))
        left_all.append(jnp.stack(lefts))
        right_kv_all.append(jnp.stack(kv_list))
        precond_all.append(conds)
    graft_blocks = graft.reshape(B, N_MP, shard_cols)
    graft_sq = jnp.stack([jnp.sum(jnp.square(graft_blocks[:, :, offset:offset + extent])) for offset, extent in spans])
    shampoo_sq = jnp.stack([sum((jnp.sum(jnp.square(precond_all[shard][number])) for shard in range(N_MP))) for number in range(3)])
    scale = jnp.sqrt(graft_sq / (shampoo_sq + norm_eps))
    pieces = []
    for shard in range(N_MP):
        for number in range(3):
            pieces.append(scale[number] * precond_all[shard][number])
    direction = jnp.concatenate(pieces, axis=1).astype(jnp.bfloat16)
    return (direction, jnp.stack(left_all), jnp.stack(right_q_all), jnp.stack(right_kv_all), moment_new)
```

```python
import jax
import jax.numpy as jnp
from jax import lax
from jax.experimental import pallas as pl
from jax.experimental.pallas import tpu as pltpu
from jax.sharding import PartitionSpec as P

MESH = pl.DeviceIdType.MESH
f32 = jnp.float32
bf16 = jnp.bfloat16

factor_keep = 0.95
factor_add = 0.05
moment_keep = 0.99
moment_add = 0.01
graft_eps = 1e-08
norm_eps = 1e-06

SIDE = 4
HALF = 16
QC = 512
KC = 64
COLS = QC + 2 * KC
ORDER = 1024
PANEL = 32
FAR_FIRST = (2, 1, 3)


def dot(a, b, ca=1, cb=0):
    return lax.dot_general(a, b, (((ca,), (cb,)), ((), ())), preferred_element_type=f32)


def kernel(
    depth,
    g, lf, lr, rq, rkv, rqr, rkvr, mom,
    gathered, scale_row, left_new, rq_new, rkv_new, mom_new,
    own, sib, part, relayed, recv1, acc, part2, recv2, total,
    lf_v, lr_v, rq_v, rkv_v, rqr_v, rkvr_v, mom_v,
    diag, slab, norm, norm_in, norm_z,
    ssem, rsem, lsem,
):
    dp = lax.axis_index("dp")
    z = lax.axis_index("mp")
    core = lax.rem(dp, 2)
    other = 1 - core
    y = lax.rem(dp // 2, SIDE)
    x = dp // (2 * SIDE)

    def at(i, j, k):
        return ((i * SIDE + j) * 2 + k, z)

    sibling = at(x, y, other)
    xs = [x] + [lax.rem(x + k, SIDE) for k in range(1, SIDE)]
    ys = [y] + [lax.rem(y + k, SIDE) for k in range(1, SIDE)]
    on_x = [None] + [at(xs[k], y, core) for k in range(1, SIDE)]
    on_y = [None] + [at(x, ys[k], core) for k in range(1, SIDE)]
    first = (on_x, on_y)
    second = (on_y, on_x)
    on_z = [None] + [(dp, lax.rem(z + k, depth)) for k in range(1, depth)]

    started = []
    local = []

    def send(src, dst, device):
        i = len(started)
        copy = pltpu.make_async_remote_copy(
            src_ref=src, dst_ref=dst, send_sem=ssem.at[i], recv_sem=rsem.at[i],
            device_id=device, device_id_type=MESH,
        )
        copy.start()
        started.append(copy)
        return copy

    def load(src, dst):
        copy = pltpu.make_async_copy(src, dst, lsem.at[len(local)])
        copy.start()
        local.append(copy)
        return copy

    def group(ref, h, k, c):
        return ref.at[xs[k], :, c, 0] if h == 0 else ref.at[:, ys[k], c, 1]

    order0 = FAR_FIRST + (0,)
    mine = {(h, k): load(group(g, h, k, core), own.at[h, k]) for k in order0 for h in range(2)}

    barrier = pltpu.get_barrier_semaphore()
    partners = [sibling] + on_x[1:] + on_y[1:] + on_z[1:]
    for device in partners:
        pl.semaphore_signal(barrier, inc=1, device_id=device, device_id_type=MESH)
    pl.semaphore_wait(barrier, len(partners))

    pair = {(h, k): send(group(g, h, k, other), sib.at[h, k], sibling) for k in order0 for h in range(2)}

    mom_load = load(mom, mom_v)
    lr_load = load(lr, lr_v)
    rqr_load = load(rqr, rqr_v)
    rkvr_load = load(rkvr, rkvr_v)
    rest = [load(lf, lf_v), load(rq, rq_v), load(rkv, rkv_v)]

    def pair_sum(h, k, part_of):
        return own[h, k, part_of].astype(f32) + sib[h, k, part_of].astype(f32)

    low, high = slice(0, 2), slice(2, 4)
    ahead, behind = 1, SIDE - 1
    relay = {}
    for h in range(2):
        mine[h, 2].wait()
        pair[h, 2].wait_recv()
        part[h, 2] = pair_sum(h, 2, slice(0, 4)).astype(bf16)
        relay[h, 0] = send(part.at[h, 2, low], relayed.at[h, 0], first[h][ahead])
        relay[h, 1] = send(part.at[h, 2, high], relayed.at[h, 1], first[h][behind])
    near = []
    for h in range(2):
        for side, k, free in ((0, ahead, high), (1, behind, low)):
            mine[h, k].wait()
            pair[h, k].wait_recv()
            part[h, k, free] = pair_sum(h, k, free).astype(bf16)
            near.append(send(part.at[h, k, free], recv1.at[h, side, free], first[h][k]))
    for h in range(2):
        for side, k, held in ((0, ahead, low), (1, behind, high)):
            relay[h, side].wait_recv()
            value = pair_sum(h, k, held) + relayed[h, side].astype(f32)
            part[h, k, held] = value.astype(bf16)
            near.append(send(part.at[h, k, held], recv1.at[h, side, held], first[h][k]))
    for h in range(2):
        mine[h, 0].wait()
        pair[h, 0].wait_recv()
        acc[h] = pair_sum(h, 0, slice(0, 4))
    for copy in near:
        copy.wait_recv()

    def line_sum(h, k):
        j = (ys if h == 0 else xs)[k]
        return acc[h, j] + recv1[h, 0, j].astype(f32) + recv1[h, 1, j].astype(f32)

    step2 = {}
    for k in FAR_FIRST:
        for h in range(2):
            part2[h, k - 1] = line_sum(h, k).astype(bf16)
            step2[h, k] = send(part2.at[h, k - 1], recv2.at[h, k - 1], second[h][k])
    for h in range(2):
        value = line_sum(h, 0)
        for k in FAR_FIRST:
            step2[h, k].wait_recv()
        for i in range(SIDE - 1):
            value = value + recv2[h, i].astype(f32)
        total[x, y, core, h] = value.astype(bf16)

    def one(ref, h, p, r):
        return ref.at[xs[p], ys[r], core, 0] if h == 0 else ref.at[xs[r], ys[p], core, 1]

    def gather(ref, hooks):
        across = {}
        along = {}
        onward = {}
        forwards = []
        halves = range(2)

        def spread(h, r):
            block = one(ref, h, 0, r)
            for p in (ahead, behind):
                along[h, p, r] = send(block, block, first[h][p])

        def pass_on(h, p, r):
            block = one(ref, h, SIDE - p, r)
            onward[h, p, r] = send(block, block, first[h][p])

        def hand_over(h, p):
            block = group(ref, h, p, core)
            forwards.append(send(block, block, sibling))

        for k in FAR_FIRST:
            for h in halves:
                block = one(ref, h, 0, 0)
                across[h, k] = send(block, block, second[h][k])
        for h in halves:
            spread(h, 0)
        hooks[0]()
        for k in (ahead, behind):
            for h in halves:
                across[h, k].wait_recv()
                spread(h, SIDE - k)
        hooks[1]()
        for h in halves:
            along[h, ahead, 0].wait_recv()
            pass_on(h, ahead, 0)
        for h in halves:
            across[h, 2].wait_recv()
            spread(h, 2)
        hooks[2]()
        for h in halves:
            hand_over(h, 0)
        for r in (behind, ahead):
            for h in halves:
                along[h, behind, r].wait_recv()
                pass_on(h, behind, r)
        hooks[3]()
        for h in halves:
            along[h, ahead, 2].wait_recv()
            pass_on(h, ahead, 2)
        for h in halves:
            for r in (ahead, behind):
                along[h, ahead, r].wait_recv()
            hand_over(h, behind)
        for h in halves:
            for r in (0, 2):
                along[h, behind, r].wait_recv()
            hand_over(h, ahead)
        hooks[4]()
        for h in halves:
            for p, r in ((ahead, 0), (behind, behind), (behind, ahead), (ahead, 2)):
                onward[h, p, r].wait_recv()
            hand_over(h, 2)
        hooks[5]()
        for copy in forwards:
            copy.wait_recv()

    lane = lax.broadcasted_iota(jnp.int32, (1, 2 * KC), 1)
    is_key = lane < KC

    def to_lanes(square):
        column = jnp.sum(square, axis=0, keepdims=True)
        query = column[:, :128]
        for i in range(1, QC // 128):
            query = query + column[:, 128 * i : 128 * (i + 1)]
        return query, column[:, QC:]

    saved = {}

    def graft_part():
        mom_load.wait()
        row_grad = total[x, y, core].reshape(PANEL, COLS).astype(f32)
        moment_new = moment_keep * mom_v[...] + moment_add * row_grad * row_grad
        mom_new[...] = moment_new
        graft = row_grad / (jnp.sqrt(moment_new) + graft_eps)
        graft_q, graft_kv = to_lanes(jnp.square(graft))
        norm[0] = jnp.zeros((8, 128), f32)
        norm[0, 0:1, :] = graft_q
        norm[0, 1:2, :] = graft_kv

    def diagonal_part():
        rkvr_load.wait()
        row = lax.broadcasted_iota(jnp.int32, (KC, 2 * KC), 0)
        col = lax.broadcasted_iota(jnp.int32, (KC, 2 * KC), 1)
        for i in range(2):
            place = (col == row + i * KC).astype(f32).astype(bf16)
            diag[KC * i : KC * (i + 1), :] = dot(rkvr_v[i], place).astype(bf16)

    def nothing():
        pass

    def wait_loads():
        lr_load.wait()
        rqr_load.wait()
        for copy in rest:
            copy.wait()

    gather(total, (graft_part, diagonal_part, nothing, wait_loads, nothing, nothing))

    grad_q = total[..., :QC].reshape(ORDER, QC)
    grad_kv = total[..., QC:].reshape(ORDER, 2 * KC)
    proj_q = dot(lr_v[0], grad_q).astype(bf16)
    both = dot(lr_v[1:3].reshape(2 * PANEL, ORDER), grad_kv)
    proj_kv = jnp.where(is_key, both[:PANEL], both[PANEL:]).astype(bf16)
    cond_q = dot(proj_q, rqr_v[...])
    cond_kv = dot(proj_kv, diag[...])
    gathered[x, y, core, :, :, :QC] = cond_q.astype(bf16).reshape(2, HALF, QC)
    gathered[x, y, core, :, :, QC:] = cond_kv.astype(bf16).reshape(2, HALF, 2 * KC)

    def norm_start():
        square = jnp.square(jnp.concatenate([cond_q, cond_kv], axis=1))
        cond_lanes_q, cond_lanes_kv = to_lanes(square)
        norm[0, 2:3, :] = cond_lanes_q
        norm[0, 3:4, :] = cond_lanes_kv
        saved["y"] = [send(norm.at[0], norm_in.at[k - 1], on_y[k]) for k in FAR_FIRST]
        left_kv()

    def left_kv():
        owned_kv = total[x, y, core].reshape(PANEL, COLS)[:, QC:].astype(f32)
        split = jnp.concatenate(
            [jnp.where(is_key, owned_kv, 0.0), jnp.where(is_key, 0.0, owned_kv)], axis=0
        ).astype(bf16)
        both = dot(split, grad_kv, 1, 1)
        left_new[1] = factor_keep * lf_v[1] + factor_add * both[:PANEL]
        left_new[2] = factor_keep * lf_v[2] + factor_add * both[PANEL:]

    def norm_next():
        for copy in saved["y"]:
            copy.wait_recv()
        norm[1] = norm[0] + norm_in[0] + norm_in[1] + norm_in[2]
        saved["x"] = [send(norm.at[1], norm_in.at[2 + k], on_x[k]) for k in FAR_FIRST]

    def norm_pair():
        for copy in saved["x"]:
            copy.wait_recv()
        norm[2] = norm[1] + norm_in[3] + norm_in[4] + norm_in[5]
        saved["c"] = send(norm.at[2], norm_in.at[6], sibling)
        owned_q = total[x, y, core].reshape(PANEL, COLS)[:, :QC]
        left_new[0] = factor_keep * lf_v[0] + factor_add * dot(owned_q, grad_q, 1, 1)

    def norm_line():
        saved["c"].wait_recv()
        norm[3] = norm[2] + norm_in[6]
        saved["z"] = [send(norm.at[3], norm_z.at[k - 1], on_z[k]) for k in range(1, depth)]

    def right_q_part():
        columns = pl.ds(pl.multiple_of(x * 128, 128), 128)
        slab[...] = dot(total[..., columns].reshape(ORDER, 128), grad_q, 0, 0)
        mine_q = pl.ds(pl.multiple_of(lax.rem(dp, 2 * SIDE) * 16, 16), 16)
        rq_new[...] = factor_keep * rq_v[...] + factor_add * slab[mine_q, :]

    def right_kv_part():
        square = dot(grad_kv, grad_kv, 0, 0)
        rkv_new[0] = factor_keep * rkv_v[0] + factor_add * square[:KC, :KC]
        moved = pltpu.roll(square, KC, 1)
        rkv_new[1] = factor_keep * rkv_v[1] + factor_add * moved[KC:, :KC]

    gather(gathered, (norm_start, norm_next, norm_pair, norm_line, right_q_part, right_kv_part))

    for copy in saved["z"]:
        copy.wait_recv()
    sums = norm[3] + jnp.sum(norm_z[...], axis=0)

    def whole(row_index, mask):
        values = sums[row_index : row_index + 1, :]
        if mask is not None:
            values = jnp.where(mask, values, 0.0)
        return jnp.sum(values, axis=1, keepdims=True)

    def scale(graft_sq, shampoo_sq):
        return jnp.sqrt(graft_sq / (shampoo_sq + norm_eps))

    scale_q = scale(whole(0, None), whole(2, None))
    scale_k = scale(whole(1, is_key), whole(3, is_key))
    scale_v = scale(whole(1, lane >= KC), whole(3, lane >= KC))
    scale_row[:, :QC] = jnp.broadcast_to(scale_q, (8, QC))
    scale_row[:, QC:] = jnp.broadcast_to(jnp.where(is_key, scale_k, scale_v), (8, 2 * KC))

    assert len(started) == ssem.shape[0]
    for copy in started:
        copy.wait_send()


def finish(gathered, scale_row, left, rq, rkv, mom, direction, left_out, rq_out, rkv_out, mom_out, rows, sem):
    copies = []

    def store(src, dst):
        copy = pltpu.make_async_copy(src, dst, sem.at[len(copies)])
        copy.start()
        copies.append(copy)

    for src, dst in ((left, left_out), (mom, mom_out), (rq, rq_out), (rkv, rkv_out)):
        store(src, dst)
    height = ORDER // SIDE
    scale = scale_row[0:1, :]
    for i in range(SIDE):
        rows[i] = (gathered[i].reshape(height, COLS).astype(f32) * scale).astype(bf16)
        store(rows.at[i], direction.at[pl.ds(i * height, height)])
    for copy in copies:
        copy.wait()


def local_step(grads, left_factor, left_root, right_q, right_kv, right_q_root, right_kv_root, moment):
    depth = lax.axis_size("mp")
    grid = (SIDE, SIDE, 2, 2, HALF, COLS)
    block = (SIDE, HALF, COLS)
    n_sends = 8 + 18 + 2 * 38 + 7 + depth - 1
    hbm = pl.BlockSpec(memory_space=pltpu.HBM)
    vmem = pl.BlockSpec(memory_space=pltpu.VMEM)
    shape = jax.ShapeDtypeStruct
    gathered, scale_row, left_new, rq_new, rkv_new, mom_new = pl.pallas_call(
        lambda *refs: kernel(depth, *refs),
        out_shape=(
            shape(grid, bf16),
            shape((8, COLS), f32),
            shape((3, PANEL, ORDER), f32),
            shape((16, QC), f32),
            shape((2, KC, KC), f32),
            shape((PANEL, COLS), f32),
        ),
        in_specs=[hbm] * 8,
        out_specs=(vmem,) * 6,
        scratch_shapes=[
            pltpu.VMEM((2, SIDE) + block, bf16),
            pltpu.VMEM((2, SIDE) + block, bf16),
            pltpu.VMEM((2, SIDE) + block, bf16),
            pltpu.VMEM((2, 2, 2, HALF, COLS), bf16),
            pltpu.VMEM((2, 2) + block, bf16),
            pltpu.VMEM((2,) + block, f32),
            pltpu.VMEM((2, SIDE - 1, HALF, COLS), bf16),
            pltpu.VMEM((2, SIDE - 1, HALF, COLS), bf16),
            pltpu.VMEM(grid, bf16),
            pltpu.VMEM((3, PANEL, ORDER), f32),
            pltpu.VMEM((3, PANEL, ORDER), bf16),
            pltpu.VMEM((16, QC), f32),
            pltpu.VMEM((2, KC, KC), f32),
            pltpu.VMEM((QC, QC), bf16),
            pltpu.VMEM((2, KC, KC), bf16),
            pltpu.VMEM((PANEL, COLS), f32),
            pltpu.VMEM((2 * KC, 2 * KC), bf16),
            pltpu.VMEM((128, QC), f32),
            pltpu.VMEM((4, 8, 128), f32),
            pltpu.VMEM((7, 8, 128), f32),
            pltpu.VMEM((depth - 1, 8, 128), f32),
            pltpu.SemaphoreType.DMA((n_sends,)),
            pltpu.SemaphoreType.DMA((n_sends,)),
            pltpu.SemaphoreType.DMA((15,)),
        ],
        compiler_params=pltpu.CompilerParams(
            collective_id=0, has_side_effects=True, vmem_limit_bytes=40 * 1024 * 1024
        ),
    )(
        *(
            pltpu.with_memory_space_constraint(array, pltpu.HBM)
            for array in (
                grads.reshape(grid), left_factor[0], left_root[0], right_q[0], right_kv[0],
                right_q_root[0], right_kv_root[0], moment,
            )
        )
    )
    direction, left_new, rq_new, rkv_new, mom_new = pl.pallas_call(
        finish,
        out_shape=(
            shape((ORDER, COLS), bf16),
            shape((3, PANEL, ORDER), f32),
            shape((16, QC), f32),
            shape((2, KC, KC), f32),
            shape((PANEL, COLS), f32),
        ),
        in_specs=[vmem] * 6,
        out_specs=(hbm,) * 5,
        scratch_shapes=[
            pltpu.VMEM((SIDE, ORDER // SIDE, COLS), bf16),
            pltpu.SemaphoreType.DMA((4 + SIDE,)),
        ],
        compiler_params=pltpu.CompilerParams(vmem_limit_bytes=40 * 1024 * 1024),
    )(gathered, scale_row, left_new, rq_new, rkv_new, mom_new)
    return direction, left_new[None], rq_new[None], rkv_new[None], mom_new


def solution(mesh):
    return jax.shard_map(
        local_step,
        mesh=mesh,
        in_specs=(
            P("dp", None, "mp"),
            P("mp", None, "dp", None),
            P("mp", None, "dp", None),
            P("mp", "dp", None),
            P("mp", None, None, None),
            P("mp", None, None),
            P("mp", None, None, None),
            P("dp", "mp"),
        ),
        out_specs=(
            P(None, "mp"),
            P("mp", None, "dp", None),
            P("mp", "dp", None),
            P("mp", None, None, None),
            P("dp", "mp"),
        ),
        check_vma=False,
    )
```

```python
import jax
import jax.numpy as jnp
from jax import lax
from jax.experimental import pallas as pl
from jax.experimental.pallas import tpu as pltpu
from jax.sharding import PartitionSpec as P

MESH = pl.DeviceIdType.MESH
f32 = jnp.float32
bf16 = jnp.bfloat16

factor_keep = 0.95
factor_add = 0.05
moment_keep = 0.99
moment_add = 0.01
graft_eps = 1e-08
norm_eps = 1e-06

SIDE = 4
HALF = 16
QC = 512
KC = 64
COLS = QC + 2 * KC
ORDER = 1024
PANEL = 32
FAR_FIRST = (2, 1, 3)


def dot(a, b, ca=1, cb=0):
    return lax.dot_general(a, b, (((ca,), (cb,)), ((), ())), preferred_element_type=f32)


def kernel(
    g, lf, lr, rq, rkv, rqr, rkvr, mom,
    gathered, scale_row, left_new, rq_new, rkv_new, mom_new,
    own, sib, part, recv1, acc, part2, recv2, total,
    lf_v, lr_v, rq_v, rkv_v, rqr_v, rkvr_v, mom_v,
    diag, slab, norm, norm_in,
    ssem, rsem, lsem,
):
    dp = lax.axis_index("dp")
    z = lax.axis_index("mp")
    core = lax.rem(dp, 2)
    other = 1 - core
    y = lax.rem(dp // 2, SIDE)
    x = dp // (2 * SIDE)
    z_low = lax.rem(z, SIDE)
    z_high = z // SIDE

    def at(i, j, k):
        return ((i * SIDE + j) * 2 + k, z)

    def ring(v):
        return [v] + [lax.rem(v + k, SIDE) for k in range(1, SIDE)]

    sibling = at(x, y, other)
    xs, ys = ring(x), ring(y)
    others = range(1, SIDE)
    on_x = [None] + [at(xs[k], y, core) for k in others]
    on_y = [None] + [at(x, ys[k], core) for k in others]
    first = (on_x, on_y)
    second = (on_y, on_x)
    crossed = [at(x, ys[k], other) for k in others]
    on_low = [(dp, z_high * SIDE + v) for v in ring(z_low)[1:]]
    on_high = [(dp, v * SIDE + z_low) for v in ring(z_high)[1:]]

    barrier = pltpu.get_barrier_semaphore()
    partners = [sibling] + on_x[1:] + on_y[1:] + crossed + on_low + on_high
    for device in partners:
        pl.semaphore_signal(barrier, inc=1, device_id=device, device_id_type=MESH)

    local = []

    def load(src, dst):
        copy = pltpu.make_async_copy(src, dst, lsem.at[len(local)])
        copy.start()
        local.append(copy)
        return copy

    mine = [load(g.at[:, :, core, h], own.at[h]) for h in range(2)]
    pl.semaphore_wait(barrier, len(partners))

    sends = {}
    arrivals = {}

    def send(src, dst, device, outgoing, incoming):
        i = sends.setdefault(outgoing, len(sends))
        j = arrivals.setdefault(incoming, len(arrivals))
        pltpu.make_async_remote_copy(
            src_ref=src, dst_ref=dst, send_sem=ssem.at[i], recv_sem=rsem.at[j],
            device_id=device, device_id_type=MESH,
        ).start()

    def all_of(ref, outgoing=None, incoming=None):
        copy = pltpu.make_async_remote_copy(
            src_ref=ref, dst_ref=ref,
            send_sem=ssem.at[sends[outgoing] if outgoing else 0],
            recv_sem=rsem.at[arrivals[incoming] if incoming else 0],
            device_id=sibling, device_id_type=MESH,
        )
        if outgoing:
            copy.wait_send()
        else:
            copy.wait_recv()

    def group(ref, h, k, c):
        return ref.at[xs[k], :, c, 0] if h == 0 else ref.at[:, ys[k], c, 1]

    for h in range(2):
        send(g.at[:, :, other, h], sib.at[h], sibling, "pair", ("pair", h))

    mom_load = load(mom, mom_v)
    lr_load = load(lr, lr_v)
    rqr_load = load(rqr, rqr_v)
    rkvr_load = load(rkvr, rkvr_v)
    rest = [load(lf, lf_v), load(rq, rq_v), load(rkv, rkv_v)]

    for h in range(2):
        mine[h].wait()
        all_of(sib.at[h], incoming=("pair", h))

        def pair_sum(k):
            if h == 0:
                return own[h, xs[k]].astype(f32) + sib[h, xs[k]].astype(f32)
            return own[h, :, ys[k]].astype(f32) + sib[h, :, ys[k]].astype(f32)

        for k in FAR_FIRST:
            part[h, k - 1] = pair_sum(k).astype(bf16)
            send(part.at[h, k - 1], recv1.at[h, k - 1], first[h][k], "step1", ("step1", h))
        acc[h] = pair_sum(0)

    kept = []
    for h in range(2):
        all_of(recv1.at[h], incoming=("step1", h))

        def line_sum(k):
            j = (ys if h == 0 else xs)[k]
            value = acc[h, j]
            for i in range(SIDE - 1):
                value = value + recv1[h, i, j].astype(f32)
            return value

        for k in FAR_FIRST:
            part2[h, k - 1] = line_sum(k).astype(bf16)
            send(part2.at[h, k - 1], recv2.at[h, k - 1], second[h][k], "step2", ("step2", h))
        kept.append(line_sum(0))
    three = recv2.at[0]
    for h in range(2):
        value = kept[h]
        all_of(recv2.at[h], incoming=("step2", h))
        for i in range(SIDE - 1):
            value = value + recv2[h, i].astype(f32)
        total[x, y, core, h] = value.astype(bf16)
        for k in FAR_FIRST:
            block = total.at[x, y, core, h]
            send(block, block, second[h][k], "across0", ("across0", h))

    def gather(ref, name, early, middle, late):
        early()
        for h in range(2):
            all_of(three, incoming=("across" + name, h))
            block = group(ref, h, 0, core)
            for k in FAR_FIRST:
                send(block, block, first[h][k], "along" + name, ("along" + name, h, k))
        for h in range(2):
            block = group(ref, h, 0, core)
            send(block, block, sibling, "over" + name, "over" + name)
        middle()
        for k in (1, 3, 2):
            for h in range(2):
                block = group(ref, h, SIDE - k, core)
                all_of(block, incoming=("along" + name, h, k))
                send(block, block, sibling, "over" + name, "over" + name)
        late()
        all_of(ref.at[:, :, other], incoming="over" + name)

    lane = lax.broadcasted_iota(jnp.int32, (1, 2 * KC), 1)
    is_key = lane < KC

    def to_lanes(square):
        column = jnp.sum(square, axis=0, keepdims=True)
        query = column[:, :128]
        for i in range(1, QC // 128):
            query = query + column[:, 128 * i : 128 * (i + 1)]
        return query, column[:, QC:]

    def graft_part():
        mom_load.wait()
        row_grad = total[x, y, core].reshape(PANEL, COLS).astype(f32)
        moment_new = moment_keep * mom_v[...] + moment_add * row_grad * row_grad
        mom_new[...] = moment_new
        graft = row_grad / (jnp.sqrt(moment_new) + graft_eps)
        graft_q, graft_kv = to_lanes(jnp.square(graft))
        norm[0] = jnp.zeros((8, 128), f32)
        norm[0, 0:1, :] = graft_q
        norm[0, 1:2, :] = graft_kv

    def diagonal_part():
        rkvr_load.wait()
        row = lax.broadcasted_iota(jnp.int32, (KC, 2 * KC), 0)
        col = lax.broadcasted_iota(jnp.int32, (KC, 2 * KC), 1)
        for i in range(2):
            place = (col == row + i * KC).astype(f32).astype(bf16)
            diag[KC * i : KC * (i + 1), :] = dot(rkvr_v[i], place).astype(bf16)

    def wait_loads():
        lr_load.wait()
        rqr_load.wait()
        for copy in rest:
            copy.wait()

    gather(total, "0", graft_part, diagonal_part, wait_loads)

    def query_grad():
        return total[..., :QC].reshape(ORDER, QC)

    def key_value_grad():
        return total[..., QC:].reshape(ORDER, 2 * KC)

    proj_q = dot(lr_v[0], query_grad()).astype(bf16)
    both = dot(lr_v[1:3].reshape(2 * PANEL, ORDER), key_value_grad())
    proj_kv = jnp.where(is_key, both[:PANEL], both[PANEL:]).astype(bf16)
    cond_q = dot(proj_q, rqr_v[...])
    cond_kv = dot(proj_kv, diag[...])
    gathered[x, y, core, :, :, :QC] = cond_q.astype(bf16).reshape(2, HALF, QC)
    gathered[x, y, core, :, :, QC:] = cond_kv.astype(bf16).reshape(2, HALF, 2 * KC)
    for h in range(2):
        for k in FAR_FIRST:
            block = gathered.at[x, y, core, h]
            send(block, block, second[h][k], "across1", ("across1", h))

    levels = (
        (0, 2 * SIDE, 2 * y + core, on_y[1:] + [sibling] + crossed),
        (2 * SIDE, SIDE, x, on_x[1:]),
        (3 * SIDE, SIDE, z_low, on_low),
        (4 * SIDE, SIDE, z_high, on_high),
    )

    def norm_send(level):
        start, _, place, devices = levels[level]
        norm_in[start + place] = norm[level]
        for device in devices:
            send(norm.at[level], norm_in.at[start + place], device, "norm", ("norm", level))

    def norm_add(level):
        start, count, _, _ = levels[level]
        all_of(norm_in.at[start : start + count - 1], incoming=("norm", level))
        value = norm_in[start]
        for i in range(1, count):
            value = value + norm_in[start + i]
        return value

    def norm_step(level):
        norm[level] = norm_add(level - 1)
        norm_send(level)

    def norm_start():
        square = jnp.square(jnp.concatenate([cond_q, cond_kv], axis=1))
        cond_lanes_q, cond_lanes_kv = to_lanes(square)
        norm[0, 2:3, :] = cond_lanes_q
        norm[0, 3:4, :] = cond_lanes_kv
        norm_send(0)

    def left_part():
        owned = total[x, y, core].reshape(PANEL, COLS)
        owned_kv = owned[:, QC:].astype(f32)
        split = jnp.concatenate(
            [jnp.where(is_key, owned_kv, 0.0), jnp.where(is_key, 0.0, owned_kv)], axis=0
        ).astype(bf16)
        both = dot(split, key_value_grad(), 1, 1)
        left_new[1] = factor_keep * lf_v[1] + factor_add * both[:PANEL]
        left_new[2] = factor_keep * lf_v[2] + factor_add * both[PANEL:]
        left_new[0] = factor_keep * lf_v[0] + factor_add * dot(owned[:, :QC], query_grad(), 1, 1)

    def right_part():
        columns = pl.ds(pl.multiple_of(x * 128, 128), 128)
        slab[...] = dot(total[..., columns].reshape(ORDER, 128), query_grad(), 0, 0)
        mine_q = pl.ds(pl.multiple_of(lax.rem(dp, 2 * SIDE) * 16, 16), 16)
        rq_new[...] = factor_keep * rq_v[...] + factor_add * slab[mine_q, :]
        square = dot(key_value_grad(), key_value_grad(), 0, 0)
        rkv_new[0] = factor_keep * rkv_v[0] + factor_add * square[:KC, :KC]
        moved = pltpu.roll(square, KC, 1)
        rkv_new[1] = factor_keep * rkv_v[1] + factor_add * moved[KC:, :KC]

    def middle_part():
        norm_step(1)
        left_part()
        norm_step(2)
        right_part()
        norm_step(3)

    def scale_part():
        sums = norm_add(3)

        def whole(row_index, mask):
            values = sums[row_index : row_index + 1, :]
            if mask is not None:
                values = jnp.where(mask, values, 0.0)
            return jnp.sum(values, axis=1, keepdims=True)

        def scale(graft_sq, shampoo_sq):
            return jnp.sqrt(graft_sq / (shampoo_sq + norm_eps))

        scale_q = scale(whole(0, None), whole(2, None))
        scale_k = scale(whole(1, is_key), whole(3, is_key))
        scale_v = scale(whole(1, lane >= KC), whole(3, lane >= KC))
        scale_row[:, :QC] = jnp.broadcast_to(scale_q, (8, QC))
        scale_row[:, QC:] = jnp.broadcast_to(jnp.where(is_key, scale_k, scale_v), (8, 2 * KC))

    gather(gathered, "1", norm_start, middle_part, scale_part)

    all_of(sib, outgoing="pair")
    all_of(recv1, outgoing="step1")
    all_of(recv2, outgoing="step2")
    for name, ref in (("0", total), ("1", gathered)):
        all_of(recv2, outgoing="across" + name)
        all_of(recv1, outgoing="along" + name)
        all_of(ref.at[:, :, core], outgoing="over" + name)
    all_of(norm_in.at[: 4 * SIDE], outgoing="norm")
    assert len(sends) == ssem.shape[0] and len(arrivals) == rsem.shape[0]


def finish(gathered, scale_row, left, rq, rkv, mom, direction, left_out, rq_out, rkv_out, mom_out, rows, sem):
    copies = []

    def store(src, dst):
        copy = pltpu.make_async_copy(src, dst, sem.at[len(copies)])
        copy.start()
        copies.append(copy)

    for src, dst in ((left, left_out), (mom, mom_out), (rq, rq_out), (rkv, rkv_out)):
        store(src, dst)
    height = ORDER // SIDE
    scale = scale_row[0:1, :]
    for i in range(SIDE):
        rows[i] = (gathered[i].reshape(height, COLS).astype(f32) * scale).astype(bf16)
        store(rows.at[i], direction.at[pl.ds(i * height, height)])
    for copy in copies:
        copy.wait()


def local_step(grads, left_factor, left_root, right_q, right_kv, right_q_root, right_kv_root, moment):
    grid = (SIDE, SIDE, 2, 2, HALF, COLS)
    block = (SIDE, HALF, COLS)
    hbm = pl.BlockSpec(memory_space=pltpu.HBM)
    vmem = pl.BlockSpec(memory_space=pltpu.VMEM)
    shape = jax.ShapeDtypeStruct
    gathered, scale_row, left_new, rq_new, rkv_new, mom_new = pl.pallas_call(
        kernel,
        out_shape=(
            shape(grid, bf16),
            shape((8, COLS), f32),
            shape((3, PANEL, ORDER), f32),
            shape((16, QC), f32),
            shape((2, KC, KC), f32),
            shape((PANEL, COLS), f32),
        ),
        in_specs=[hbm] * 8,
        out_specs=(vmem,) * 6,
        scratch_shapes=[
            pltpu.VMEM((2, SIDE) + block, bf16),
            pltpu.VMEM((2, SIDE) + block, bf16),
            pltpu.VMEM((2, SIDE - 1) + block, bf16),
            pltpu.VMEM((2, SIDE - 1) + block, bf16),
            pltpu.VMEM((2,) + block, f32),
            pltpu.VMEM((2, SIDE - 1, HALF, COLS), bf16),
            pltpu.VMEM((2, SIDE - 1, HALF, COLS), bf16),
            pltpu.VMEM(grid, bf16),
            pltpu.VMEM((3, PANEL, ORDER), f32),
            pltpu.VMEM((3, PANEL, ORDER), bf16),
            pltpu.VMEM((16, QC), f32),
            pltpu.VMEM((2, KC, KC), f32),
            pltpu.VMEM((QC, QC), bf16),
            pltpu.VMEM((2, KC, KC), bf16),
            pltpu.VMEM((PANEL, COLS), f32),
            pltpu.VMEM((2 * KC, 2 * KC), bf16),
            pltpu.VMEM((128, QC), f32),
            pltpu.VMEM((4, 8, 128), f32),
            pltpu.VMEM((5 * SIDE, 8, 128), f32),
            pltpu.SemaphoreType.DMA((10,)),
            pltpu.SemaphoreType.DMA((28,)),
            pltpu.SemaphoreType.DMA((9,)),
        ],
        compiler_params=pltpu.CompilerParams(
            collective_id=0, has_side_effects=True, vmem_limit_bytes=40 * 1024 * 1024
        ),
    )(
        *(
            pltpu.with_memory_space_constraint(array, pltpu.HBM)
            for array in (
                grads.reshape(grid), left_factor[0], left_root[0], right_q[0], right_kv[0],
                right_q_root[0], right_kv_root[0], moment,
            )
        )
    )
    direction, left_new, rq_new, rkv_new, mom_new = pl.pallas_call(
        finish,
        out_shape=(
            shape((ORDER, COLS), bf16),
            shape((3, PANEL, ORDER), f32),
            shape((16, QC), f32),
            shape((2, KC, KC), f32),
            shape((PANEL, COLS), f32),
        ),
        in_specs=[vmem] * 6,
        out_specs=(hbm,) * 5,
        scratch_shapes=[
            pltpu.VMEM((SIDE, ORDER // SIDE, COLS), bf16),
            pltpu.SemaphoreType.DMA((4 + SIDE,)),
        ],
        compiler_params=pltpu.CompilerParams(vmem_limit_bytes=40 * 1024 * 1024),
    )(gathered, scale_row, left_new, rq_new, rkv_new, mom_new)
    return direction, left_new[None], rq_new[None], rkv_new[None], mom_new


def solution(mesh):
    return jax.shard_map(
        local_step,
        mesh=mesh,
        in_specs=(
            P("dp", None, "mp"),
            P("mp", None, "dp", None),
            P("mp", None, "dp", None),
            P("mp", "dp", None),
            P("mp", None, None, None),
            P("mp", None, None),
            P("mp", None, None, None),
            P("dp", "mp"),
        ),
        out_specs=(
            P(None, "mp"),
            P("mp", None, "dp", None),
            P("mp", "dp", None),
            P("mp", None, None, None),
            P("dp", "mp"),
        ),
        check_vma=False,
    )
```

```python
import jax
import jax.numpy as jnp
from jax import lax
from jax.experimental import pallas as pl
from jax.experimental.pallas import tpu as pltpu
from jax.sharding import PartitionSpec as P

MESH = pl.DeviceIdType.MESH
f32 = jnp.float32
bf16 = jnp.bfloat16

factor_keep = 0.95
factor_add = 0.05
moment_keep = 0.99
moment_add = 0.01
graft_eps = 1e-08
norm_eps = 1e-06

SIDE = 4
HALF = 16
QC = 512
KC = 64
COLS = QC + 2 * KC
ORDER = 1024
PANEL = 32
FAR_FIRST = (2, 1, 3)


def dot(a, b, ca=1, cb=0):
    return lax.dot_general(a, b, (((ca,), (cb,)), ((), ())), preferred_element_type=f32)


def kernel(
    g, lr, rqr, rkvr, mom,
    gathered, total, scale_row, mom_new,
    own, sib, part, recv1, acc, part2, recv2,
    lr_v, rqr_v, rkvr_v, mom_v,
    diag, norm, norm_in,
    ssem, rsem, lsem,
):
    dp = lax.axis_index("dp")
    z = lax.axis_index("mp")
    core = lax.rem(dp, 2)
    other = 1 - core
    y = lax.rem(dp // 2, SIDE)
    x = dp // (2 * SIDE)
    z_low = lax.rem(z, SIDE)
    z_high = z // SIDE

    def at(i, j, k):
        return ((i * SIDE + j) * 2 + k, z)

    def ring(v):
        return [v] + [lax.rem(v + k, SIDE) for k in range(1, SIDE)]

    sibling = at(x, y, other)
    xs, ys = ring(x), ring(y)
    others = range(1, SIDE)
    on_x = [None] + [at(xs[k], y, core) for k in others]
    on_y = [None] + [at(x, ys[k], core) for k in others]
    first = (on_x, on_y)
    second = (on_y, on_x)
    crossed = [at(x, ys[k], other) for k in others]
    on_low = [(dp, z_high * SIDE + v) for v in ring(z_low)[1:]]
    on_high = [(dp, v * SIDE + z_low) for v in ring(z_high)[1:]]

    barrier = pltpu.get_barrier_semaphore()
    partners = [sibling] + on_x[1:] + on_y[1:] + crossed + on_low + on_high
    for device in partners:
        pl.semaphore_signal(barrier, inc=1, device_id=device, device_id_type=MESH)

    local = []

    def load(src, dst):
        copy = pltpu.make_async_copy(src, dst, lsem.at[len(local)])
        copy.start()
        local.append(copy)
        return copy

    mine = [load(g.at[:, :, core, h], own.at[h]) for h in range(2)]
    pl.semaphore_wait(barrier, len(partners))

    sends = {}
    arrivals = {}

    def send(src, dst, device, outgoing, incoming):
        i = sends.setdefault(outgoing, len(sends))
        j = arrivals.setdefault(incoming, len(arrivals))
        pltpu.make_async_remote_copy(
            src_ref=src, dst_ref=dst, send_sem=ssem.at[i], recv_sem=rsem.at[j],
            device_id=device, device_id_type=MESH,
        ).start()

    def all_of(ref, outgoing=None, incoming=None):
        copy = pltpu.make_async_remote_copy(
            src_ref=ref, dst_ref=ref,
            send_sem=ssem.at[sends[outgoing] if outgoing else 0],
            recv_sem=rsem.at[arrivals[incoming] if incoming else 0],
            device_id=sibling, device_id_type=MESH,
        )
        if outgoing:
            copy.wait_send()
        else:
            copy.wait_recv()

    def group(ref, h, k, c):
        return ref.at[xs[k], :, c, 0] if h == 0 else ref.at[:, ys[k], c, 1]

    for h in range(2):
        send(g.at[:, :, other, h], sib.at[h], sibling, "pair", ("pair", h))

    mom_load = load(mom, mom_v)
    lr_load = load(lr, lr_v)
    rqr_load = load(rqr, rqr_v)
    rkvr_load = load(rkvr, rkvr_v)

    for h in range(2):
        mine[h].wait()
        all_of(sib.at[h], incoming=("pair", h))

        def pair_sum(k):
            if h == 0:
                return own[h, xs[k]].astype(f32) + sib[h, xs[k]].astype(f32)
            return own[h, :, ys[k]].astype(f32) + sib[h, :, ys[k]].astype(f32)

        for k in FAR_FIRST:
            part[h, k - 1] = pair_sum(k).astype(bf16)
            send(part.at[h, k - 1], recv1.at[h, k - 1], first[h][k], "step1", ("step1", h))
        acc[h] = pair_sum(0)

    kept = []
    for h in range(2):
        all_of(recv1.at[h], incoming=("step1", h))

        def line_sum(k):
            j = (ys if h == 0 else xs)[k]
            value = acc[h, j]
            for i in range(SIDE - 1):
                value = value + recv1[h, i, j].astype(f32)
            return value

        for k in FAR_FIRST:
            part2[h, k - 1] = line_sum(k).astype(bf16)
            send(part2.at[h, k - 1], recv2.at[h, k - 1], second[h][k], "step2", ("step2", h))
        kept.append(line_sum(0))
    three = recv2.at[0]
    for h in range(2):
        value = kept[h]
        all_of(recv2.at[h], incoming=("step2", h))
        for i in range(SIDE - 1):
            value = value + recv2[h, i].astype(f32)
        total[x, y, core, h] = value.astype(bf16)
        for k in FAR_FIRST:
            block = total.at[x, y, core, h]
            send(block, block, second[h][k], "across0", ("across0", h))

    def gather(ref, name, early, middle, late):
        early()
        for h in range(2):
            all_of(three, incoming=("across" + name, h))
            block = group(ref, h, 0, core)
            for k in FAR_FIRST:
                send(block, block, first[h][k], "along" + name, ("along" + name, h, k))
        for h in range(2):
            block = group(ref, h, 0, core)
            send(block, block, sibling, "over" + name, "over" + name)
        middle()
        for k in (1, 3, 2):
            for h in range(2):
                block = group(ref, h, SIDE - k, core)
                all_of(block, incoming=("along" + name, h, k))
                send(block, block, sibling, "over" + name, "over" + name)
        late()
        all_of(ref.at[:, :, other], incoming="over" + name)

    lane = lax.broadcasted_iota(jnp.int32, (1, 2 * KC), 1)
    is_key = lane < KC

    def to_lanes(square):
        column = jnp.sum(square, axis=0, keepdims=True)
        query = column[:, :128]
        for i in range(1, QC // 128):
            query = query + column[:, 128 * i : 128 * (i + 1)]
        return query, column[:, QC:]

    def graft_part():
        mom_load.wait()
        row_grad = total[x, y, core].reshape(PANEL, COLS).astype(f32)
        moment_new = moment_keep * mom_v[...] + moment_add * row_grad * row_grad
        mom_new[...] = moment_new
        graft = row_grad / (jnp.sqrt(moment_new) + graft_eps)
        graft_q, graft_kv = to_lanes(jnp.square(graft))
        norm[0] = jnp.zeros((8, 128), f32)
        norm[0, 0:1, :] = graft_q
        norm[0, 1:2, :] = graft_kv

    def diagonal_part():
        rkvr_load.wait()
        row = lax.broadcasted_iota(jnp.int32, (KC, 2 * KC), 0)
        col = lax.broadcasted_iota(jnp.int32, (KC, 2 * KC), 1)
        for i in range(2):
            place = (col == row + i * KC).astype(f32).astype(bf16)
            diag[KC * i : KC * (i + 1), :] = dot(rkvr_v[i], place).astype(bf16)

    def wait_loads():
        lr_load.wait()
        rqr_load.wait()

    gather(total, "0", graft_part, diagonal_part, wait_loads)

    def query_grad():
        return total[..., :QC].reshape(ORDER, QC)

    def key_value_grad():
        return total[..., QC:].reshape(ORDER, 2 * KC)

    proj_q = dot(lr_v[0], query_grad()).astype(bf16)
    both = dot(lr_v[1:3].reshape(2 * PANEL, ORDER), key_value_grad())
    proj_kv = jnp.where(is_key, both[:PANEL], both[PANEL:]).astype(bf16)
    cond_q = dot(proj_q, rqr_v[...])
    cond_kv = dot(proj_kv, diag[...])
    gathered[x, y, core, :, :, :QC] = cond_q.astype(bf16).reshape(2, HALF, QC)
    gathered[x, y, core, :, :, QC:] = cond_kv.astype(bf16).reshape(2, HALF, 2 * KC)
    for h in range(2):
        for k in FAR_FIRST:
            block = gathered.at[x, y, core, h]
            send(block, block, second[h][k], "across1", ("across1", h))

    levels = (
        (0, 2 * SIDE, 2 * y + core, on_y[1:] + [sibling] + crossed),
        (2 * SIDE, SIDE, x, on_x[1:]),
        (3 * SIDE, SIDE, z_low, on_low),
        (4 * SIDE, SIDE, z_high, on_high),
    )

    def norm_send(level):
        start, _, place, devices = levels[level]
        norm_in[start + place] = norm[level]
        for device in devices:
            send(norm.at[level], norm_in.at[start + place], device, "norm", ("norm", level))

    def norm_add(level):
        start, count, _, _ = levels[level]
        all_of(norm_in.at[start : start + count - 1], incoming=("norm", level))
        value = norm_in[start]
        for i in range(1, count):
            value = value + norm_in[start + i]
        return value

    def norm_step(level):
        norm[level] = norm_add(level - 1)
        norm_send(level)

    def norm_start():
        square = jnp.square(jnp.concatenate([cond_q, cond_kv], axis=1))
        cond_lanes_q, cond_lanes_kv = to_lanes(square)
        norm[0, 2:3, :] = cond_lanes_q
        norm[0, 3:4, :] = cond_lanes_kv
        norm_send(0)

    def middle_part():
        norm_step(1)
        norm_step(2)
        norm_step(3)

    def scale_part():
        sums = norm_add(3)

        def whole(row_index, mask):
            values = sums[row_index : row_index + 1, :]
            if mask is not None:
                values = jnp.where(mask, values, 0.0)
            return jnp.sum(values, axis=1, keepdims=True)

        def scale(graft_sq, shampoo_sq):
            return jnp.sqrt(graft_sq / (shampoo_sq + norm_eps))

        scale_q = scale(whole(0, None), whole(2, None))
        scale_k = scale(whole(1, is_key), whole(3, is_key))
        scale_v = scale(whole(1, lane >= KC), whole(3, lane >= KC))
        scale_row[:, :QC] = jnp.broadcast_to(scale_q, (8, QC))
        scale_row[:, QC:] = jnp.broadcast_to(jnp.where(is_key, scale_k, scale_v), (8, 2 * KC))

    gather(gathered, "1", norm_start, middle_part, scale_part)

    all_of(sib, outgoing="pair")
    all_of(recv1, outgoing="step1")
    all_of(recv2, outgoing="step2")
    for name, ref in (("0", total), ("1", gathered)):
        all_of(recv2, outgoing="across" + name)
        all_of(recv1, outgoing="along" + name)
        all_of(ref.at[:, :, core], outgoing="over" + name)
    all_of(norm_in.at[: 4 * SIDE], outgoing="norm")
    assert len(sends) == ssem.shape[0] and len(arrivals) == rsem.shape[0]


def finish(
    gathered, total, scale_row, mom, lf, rq, rkv,
    direction, left_out, rq_out, rkv_out, mom_out,
    rows, lf_v, rq_v, rkv_v, slab, sem,
):
    dp = lax.axis_index("dp")
    x = dp // (2 * SIDE)
    place = lax.rem(dp, 2 * SIDE)
    count = [0]

    def copy(src, dst):
        made = pltpu.make_async_copy(src, dst, sem.at[count[0]])
        count[0] += 1
        made.start()
        return made

    loads = [copy(lf, lf_v), copy(rq, rq_v), copy(rkv, rkv_v)]
    stores = [copy(mom, mom_out)]
    height = ORDER // SIDE
    scale = scale_row[0:1, :]
    for i in range(SIDE):
        rows[i] = (gathered[i].reshape(height, COLS).astype(f32) * scale).astype(bf16)
        stores.append(copy(rows.at[i], direction.at[pl.ds(i * height, height)]))

    def query_grad():
        return total[..., :QC].reshape(ORDER, QC)

    def key_value_grad():
        return total[..., QC:].reshape(ORDER, 2 * KC)

    for made in loads:
        made.wait()
    is_key = lax.broadcasted_iota(jnp.int32, (1, 2 * KC), 1) < KC
    owned = total[x, place // 2, lax.rem(place, 2)].reshape(PANEL, COLS)
    owned_kv = owned[:, QC:].astype(f32)
    split = jnp.concatenate(
        [jnp.where(is_key, owned_kv, 0.0), jnp.where(is_key, 0.0, owned_kv)], axis=0
    ).astype(bf16)
    lf_v[0] = factor_keep * lf_v[0] + factor_add * dot(owned[:, :QC], query_grad(), 1, 1)
    both = dot(split, key_value_grad(), 1, 1)
    lf_v[1] = factor_keep * lf_v[1] + factor_add * both[:PANEL]
    lf_v[2] = factor_keep * lf_v[2] + factor_add * both[PANEL:]
    stores.append(copy(lf_v, left_out))

    columns = pl.ds(pl.multiple_of(x * 128, 128), 128)
    slab[...] = dot(total[..., columns].reshape(ORDER, 128), query_grad(), 0, 0)
    mine_q = pl.ds(pl.multiple_of(place * 16, 16), 16)
    rq_v[...] = factor_keep * rq_v[...] + factor_add * slab[mine_q, :]
    stores.append(copy(rq_v, rq_out))
    square = dot(key_value_grad(), key_value_grad(), 0, 0)
    rkv_v[0] = factor_keep * rkv_v[0] + factor_add * square[:KC, :KC]
    moved = pltpu.roll(square, KC, 1)
    rkv_v[1] = factor_keep * rkv_v[1] + factor_add * moved[KC:, :KC]
    stores.append(copy(rkv_v, rkv_out))
    for made in stores:
        made.wait()


def local_step(grads, left_factor, left_root, right_q, right_kv, right_q_root, right_kv_root, moment):
    grid = (SIDE, SIDE, 2, 2, HALF, COLS)
    block = (SIDE, HALF, COLS)
    hbm = pl.BlockSpec(memory_space=pltpu.HBM)
    vmem = pl.BlockSpec(memory_space=pltpu.VMEM)
    shape = jax.ShapeDtypeStruct

    def stay(*arrays):
        return tuple(pltpu.with_memory_space_constraint(array, pltpu.HBM) for array in arrays)

    gathered, total, scale_row, mom_new = pl.pallas_call(
        kernel,
        out_shape=(
            shape(grid, bf16),
            shape(grid, bf16),
            shape((8, COLS), f32),
            shape((PANEL, COLS), f32),
        ),
        in_specs=[hbm] * 5,
        out_specs=(vmem,) * 4,
        scratch_shapes=[
            pltpu.VMEM((2, SIDE) + block, bf16),
            pltpu.VMEM((2, SIDE) + block, bf16),
            pltpu.VMEM((2, SIDE - 1) + block, bf16),
            pltpu.VMEM((2, SIDE - 1) + block, bf16),
            pltpu.VMEM((2,) + block, f32),
            pltpu.VMEM((2, SIDE - 1, HALF, COLS), bf16),
            pltpu.VMEM((2, SIDE - 1, HALF, COLS), bf16),
            pltpu.VMEM((3, PANEL, ORDER), bf16),
            pltpu.VMEM((QC, QC), bf16),
            pltpu.VMEM((2, KC, KC), bf16),
            pltpu.VMEM((PANEL, COLS), f32),
            pltpu.VMEM((2 * KC, 2 * KC), bf16),
            pltpu.VMEM((4, 8, 128), f32),
            pltpu.VMEM((5 * SIDE, 8, 128), f32),
            pltpu.SemaphoreType.DMA((10,)),
            pltpu.SemaphoreType.DMA((28,)),
            pltpu.SemaphoreType.DMA((6,)),
        ],
        compiler_params=pltpu.CompilerParams(
            collective_id=0, has_side_effects=True, vmem_limit_bytes=40 * 1024 * 1024
        ),
    )(*stay(grads.reshape(grid), left_root[0], right_q_root[0], right_kv_root[0], moment))
    direction, left_new, rq_new, rkv_new, mom_new = pl.pallas_call(
        finish,
        out_shape=(
            shape((ORDER, COLS), bf16),
            shape((3, PANEL, ORDER), f32),
            shape((16, QC), f32),
            shape((2, KC, KC), f32),
            shape((PANEL, COLS), f32),
        ),
        in_specs=[vmem] * 4 + [hbm] * 3,
        out_specs=(hbm,) * 5,
        scratch_shapes=[
            pltpu.VMEM((SIDE, ORDER // SIDE, COLS), bf16),
            pltpu.VMEM((3, PANEL, ORDER), f32),
            pltpu.VMEM((16, QC), f32),
            pltpu.VMEM((2, KC, KC), f32),
            pltpu.VMEM((128, QC), f32),
            pltpu.SemaphoreType.DMA((11,)),
        ],
        compiler_params=pltpu.CompilerParams(vmem_limit_bytes=40 * 1024 * 1024),
    )(gathered, total, scale_row, mom_new, *stay(left_factor[0], right_q[0], right_kv[0]))
    return direction, left_new[None], rq_new[None], rkv_new[None], mom_new


def solution(mesh):
    return jax.shard_map(
        local_step,
        mesh=mesh,
        in_specs=(
            P("dp", None, "mp"),
            P("mp", None, "dp", None),
            P("mp", None, "dp", None),
            P("mp", "dp", None),
            P("mp", None, None, None),
            P("mp", None, None),
            P("mp", None, None, None),
            P("dp", "mp"),
        ),
        out_specs=(
            P(None, "mp"),
            P("mp", None, "dp", None),
            P("mp", "dp", None),
            P("mp", None, None, None),
            P("dp", "mp"),
        ),
        check_vma=False,
    )
```

```python
import jax
import jax.numpy as jnp
from jax import lax
from jax.experimental import pallas as pl
from jax.experimental.pallas import tpu as pltpu
from jax.sharding import PartitionSpec as P

MESH = pl.DeviceIdType.MESH
f32 = jnp.float32
bf16 = jnp.bfloat16

factor_keep = 0.95
factor_add = 0.05
moment_keep = 0.99
moment_add = 0.01
graft_eps = 1e-08
norm_eps = 1e-06

SIDE = 4
HALF = 16
QC = 512
KC = 64
COLS = QC + 2 * KC
ORDER = 1024
PANEL = 32
FAR_FIRST = (2, 1, 3)


def dot(a, b, ca=1, cb=0):
    return lax.dot_general(a, b, (((ca,), (cb,)), ((), ())), preferred_element_type=f32)


def kernel(
    g, lf, lr, rq, rkv, rqr, rkvr, mom,
    gathered, scale_row, left_new, rq_new, rkv_new, mom_new,
    own, sib, part, recv1, acc, part2, recv2, total,
    lf_v, lr_v, rq_v, rkv_v, rqr_v, rkvr_v, mom_v,
    diag, slab, norm, norm_in,
    ssem, rsem, lsem,
):
    dp = lax.axis_index("dp")
    z = lax.axis_index("mp")
    core = lax.rem(dp, 2)
    other = 1 - core
    y = lax.rem(dp // 2, SIDE)
    x = dp // (2 * SIDE)
    z_low = lax.rem(z, 2)
    z_high = z // 2
    deep = lax.axis_size("mp") // 2

    def at(i, j, k, depth=z):
        return ((i * SIDE + j) * 2 + k, depth)

    def ring(v):
        return [v] + [lax.rem(v + k, SIDE) for k in range(1, SIDE)]

    sibling = at(x, y, other)
    xs, ys = ring(x), ring(y)
    others = range(1, SIDE)
    on_x = [None] + [at(xs[k], y, core) for k in others]
    on_y = [None] + [at(x, ys[k], core) for k in others]
    first = (on_x, on_y)
    second = (on_y, on_x)
    crossed = [at(x, ys[k], other) for k in others]
    slanted = [at(v, y, core, 2 * z_high + 1 - z_low) for v in xs]
    on_high = [(dp, 2 * lax.rem(z_high + k, deep) + z_low) for k in range(1, deep)]

    barrier = pltpu.get_barrier_semaphore()
    partners = [sibling] + on_x[1:] + on_y[1:] + crossed + slanted + on_high
    for device in partners:
        pl.semaphore_signal(barrier, inc=1, device_id=device, device_id_type=MESH)

    local = []

    def load(src, dst):
        copy = pltpu.make_async_copy(src, dst, lsem.at[len(local)])
        copy.start()
        local.append(copy)
        return copy

    def group(ref, h, k, c):
        return ref.at[xs[k], :, c, 0] if h == 0 else ref.at[:, ys[k], c, 1]

    far_first = FAR_FIRST + (0,)
    mine = {(h, k): load(group(g, h, k, core), own.at[h, k]) for k in far_first for h in range(2)}
    pl.semaphore_wait(barrier, len(partners))

    sends = {}
    arrivals = {}

    def send(src, dst, device, outgoing, incoming):
        i = sends.setdefault(outgoing, len(sends))
        j = arrivals.setdefault(incoming, len(arrivals))
        pltpu.make_async_remote_copy(
            src_ref=src, dst_ref=dst, send_sem=ssem.at[i], recv_sem=rsem.at[j],
            device_id=device, device_id_type=MESH,
        ).start()

    def all_of(ref, outgoing=None, incoming=None):
        copy = pltpu.make_async_remote_copy(
            src_ref=ref, dst_ref=ref,
            send_sem=ssem.at[sends[outgoing] if outgoing else 0],
            recv_sem=rsem.at[arrivals[incoming] if incoming else 0],
            device_id=sibling, device_id_type=MESH,
        )
        if outgoing:
            copy.wait_send()
        else:
            copy.wait_recv()

    for k in far_first:
        for h in range(2):
            send(group(g, h, k, other), sib.at[h, k], sibling, "pair", ("pair", h, k))

    mom_load = load(mom, mom_v)
    lr_load = load(lr, lr_v)
    rqr_load = load(rqr, rqr_v)
    rkvr_load = load(rkvr, rkvr_v)
    rest = [load(lf, lf_v), load(rq, rq_v), load(rkv, rkv_v)]

    for k in far_first:
        for h in range(2):
            mine[h, k].wait()
            all_of(sib.at[h, k], incoming=("pair", h, k))
            pair_sum = own[h, k].astype(f32) + sib[h, k].astype(f32)
            if k:
                part[h, k - 1] = pair_sum.astype(bf16)
                send(part.at[h, k - 1], recv1.at[h, k - 1], first[h][k], "step1", ("step1", h))
            else:
                acc[h] = pair_sum

    kept = []
    for h in range(2):
        all_of(recv1.at[h], incoming=("step1", h))

        def line_sum(k):
            j = (ys if h == 0 else xs)[k]
            value = acc[h, j]
            for i in range(SIDE - 1):
                value = value + recv1[h, i, j].astype(f32)
            return value

        for k in FAR_FIRST:
            part2[h, k - 1] = line_sum(k).astype(bf16)
            send(part2.at[h, k - 1], recv2.at[h, k - 1], second[h][k], "step2", ("step2", h))
        kept.append(line_sum(0))
    three = recv2.at[0]
    for h in range(2):
        value = kept[h]
        all_of(recv2.at[h], incoming=("step2", h))
        for i in range(SIDE - 1):
            value = value + recv2[h, i].astype(f32)
        total[x, y, core, h] = value.astype(bf16)
        for k in FAR_FIRST:
            block = total.at[x, y, core, h]
            send(block, block, second[h][k], "across0", ("across0", h))

    def gather(ref, name, early, middle, late):
        early()
        for h in range(2):
            all_of(three, incoming=("across" + name, h))
            block = group(ref, h, 0, core)
            for k in FAR_FIRST:
                send(block, block, first[h][k], "along" + name, ("along" + name, h, k))
        for h in range(2):
            block = group(ref, h, 0, core)
            send(block, block, sibling, "over" + name, "over" + name)
        middle()
        for k in (1, 3, 2):
            for h in range(2):
                block = group(ref, h, SIDE - k, core)
                all_of(block, incoming=("along" + name, h, k))
                send(block, block, sibling, "over" + name, "over" + name)
        late()
        all_of(ref.at[:, :, other], incoming="over" + name)

    lane = lax.broadcasted_iota(jnp.int32, (1, 2 * KC), 1)
    is_key = lane < KC

    def to_lanes(square):
        column = jnp.sum(square, axis=0, keepdims=True)
        query = column[:, :128]
        for i in range(1, QC // 128):
            query = query + column[:, 128 * i : 128 * (i + 1)]
        return query, column[:, QC:]

    def graft_part():
        mom_load.wait()
        row_grad = total[x, y, core].reshape(PANEL, COLS).astype(f32)
        moment_new = moment_keep * mom_v[...] + moment_add * row_grad * row_grad
        mom_new[...] = moment_new
        graft = row_grad / (jnp.sqrt(moment_new) + graft_eps)
        graft_q, graft_kv = to_lanes(jnp.square(graft))
        norm[0] = jnp.zeros((8, 128), f32)
        norm[0, 0:1, :] = graft_q
        norm[0, 1:2, :] = graft_kv

    def diagonal_part():
        rkvr_load.wait()
        row = lax.broadcasted_iota(jnp.int32, (KC, 2 * KC), 0)
        col = lax.broadcasted_iota(jnp.int32, (KC, 2 * KC), 1)
        for i in range(2):
            place = (col == row + i * KC).astype(f32).astype(bf16)
            diag[KC * i : KC * (i + 1), :] = dot(rkvr_v[i], place).astype(bf16)

    def wait_loads():
        lr_load.wait()
        rqr_load.wait()
        for copy in rest:
            copy.wait()

    gather(total, "0", graft_part, diagonal_part, wait_loads)

    def query_grad():
        return total[..., :QC].reshape(ORDER, QC)

    def key_value_grad():
        return total[..., QC:].reshape(ORDER, 2 * KC)

    proj_q = dot(lr_v[0], query_grad()).astype(bf16)
    both = dot(lr_v[1:3].reshape(2 * PANEL, ORDER), key_value_grad())
    proj_kv = jnp.where(is_key, both[:PANEL], both[PANEL:]).astype(bf16)
    cond_q = dot(proj_q, rqr_v[...])
    cond_kv = dot(proj_kv, diag[...])

    eight = 2 * SIDE
    levels = (
        (2 * y + core, on_y[1:] + [sibling] + crossed),
        (2 * x + z_low, on_x[1:] + slanted),
        (z_high, on_high),
    )

    def norm_send(level):
        place, devices = levels[level]
        slot = level * eight + place
        norm_in[slot] = norm[level]
        for device in devices:
            send(norm.at[level], norm_in.at[slot], device, "norm", ("norm", level))

    def norm_add(level):
        start = level * eight
        all_of(norm_in.at[start : start + eight - 1], incoming=("norm", level))
        value = norm_in[start]
        for i in range(1, eight):
            value = value + norm_in[start + i]
        return value

    def norm_step(level):
        norm[level] = norm_add(level - 1)
        norm_send(level)

    square = jnp.square(jnp.concatenate([cond_q, cond_kv], axis=1))
    cond_lanes_q, cond_lanes_kv = to_lanes(square)
    norm[0, 2:3, :] = cond_lanes_q
    norm[0, 3:4, :] = cond_lanes_kv
    norm_send(0)
    gathered[x, y, core, :, :, :QC] = cond_q.astype(bf16).reshape(2, HALF, QC)
    gathered[x, y, core, :, :, QC:] = cond_kv.astype(bf16).reshape(2, HALF, 2 * KC)
    for h in range(2):
        for k in FAR_FIRST:
            block = gathered.at[x, y, core, h]
            send(block, block, second[h][k], "across1", ("across1", h))

    def left_part():
        owned = total[x, y, core].reshape(PANEL, COLS)
        owned_kv = owned[:, QC:].astype(f32)
        split = jnp.concatenate(
            [jnp.where(is_key, owned_kv, 0.0), jnp.where(is_key, 0.0, owned_kv)], axis=0
        ).astype(bf16)
        both = dot(split, key_value_grad(), 1, 1)
        left_new[1] = factor_keep * lf_v[1] + factor_add * both[:PANEL]
        left_new[2] = factor_keep * lf_v[2] + factor_add * both[PANEL:]
        left_new[0] = factor_keep * lf_v[0] + factor_add * dot(owned[:, :QC], query_grad(), 1, 1)

    def right_part():
        columns = pl.ds(pl.multiple_of(x * 128, 128), 128)
        slab[...] = dot(total[..., columns].reshape(ORDER, 128), query_grad(), 0, 0)
        mine_q = pl.ds(pl.multiple_of(lax.rem(dp, 2 * SIDE) * 16, 16), 16)
        rq_new[...] = factor_keep * rq_v[...] + factor_add * slab[mine_q, :]
        square = dot(key_value_grad(), key_value_grad(), 0, 0)
        rkv_new[0] = factor_keep * rkv_v[0] + factor_add * square[:KC, :KC]
        moved = pltpu.roll(square, KC, 1)
        rkv_new[1] = factor_keep * rkv_v[1] + factor_add * moved[KC:, :KC]

    def early_part():
        left_part()
        norm_step(1)
        right_part()
        norm_step(2)

    def wait_rest():
        pass

    def scale_part():
        sums = norm_add(2)

        def whole(row_index, mask):
            values = sums[row_index : row_index + 1, :]
            if mask is not None:
                values = jnp.where(mask, values, 0.0)
            return jnp.sum(values, axis=1, keepdims=True)

        def scale(graft_sq, shampoo_sq):
            return jnp.sqrt(graft_sq / (shampoo_sq + norm_eps))

        scale_q = scale(whole(0, None), whole(2, None))
        scale_k = scale(whole(1, is_key), whole(3, is_key))
        scale_v = scale(whole(1, lane >= KC), whole(3, lane >= KC))
        scale_row[:, :QC] = jnp.broadcast_to(scale_q, (8, QC))
        scale_row[:, QC:] = jnp.broadcast_to(jnp.where(is_key, scale_k, scale_v), (8, 2 * KC))

    gather(gathered, "1", early_part, wait_rest, scale_part)

    all_of(sib, outgoing="pair")
    all_of(recv1, outgoing="step1")
    all_of(recv2, outgoing="step2")
    for name, ref in (("0", total), ("1", gathered)):
        all_of(recv2, outgoing="across" + name)
        all_of(recv1, outgoing="along" + name)
        all_of(ref.at[:, :, core], outgoing="over" + name)
    all_of(norm_in.at[: 3 * (eight - 1)], outgoing="norm")
    assert len(sends) == ssem.shape[0] and len(arrivals) == rsem.shape[0]


def finish(gathered, scale_row, left, rq, rkv, mom, direction, left_out, rq_out, rkv_out, mom_out, rows, sem):
    copies = []

    def store(src, dst):
        copy = pltpu.make_async_copy(src, dst, sem.at[len(copies)])
        copy.start()
        copies.append(copy)

    for src, dst in ((left, left_out), (mom, mom_out), (rq, rq_out), (rkv, rkv_out)):
        store(src, dst)
    height = ORDER // SIDE
    scale = scale_row[0:1, :]
    for i in range(SIDE):
        rows[i] = (gathered[i].reshape(height, COLS).astype(f32) * scale).astype(bf16)
        store(rows.at[i], direction.at[pl.ds(i * height, height)])
    for copy in copies:
        copy.wait()


def local_step(grads, left_factor, left_root, right_q, right_kv, right_q_root, right_kv_root, moment):
    grid = (SIDE, SIDE, 2, 2, HALF, COLS)
    block = (SIDE, HALF, COLS)
    hbm = pl.BlockSpec(memory_space=pltpu.HBM)
    vmem = pl.BlockSpec(memory_space=pltpu.VMEM)
    shape = jax.ShapeDtypeStruct
    gathered, scale_row, left_new, rq_new, rkv_new, mom_new = pl.pallas_call(
        kernel,
        out_shape=(
            shape(grid, bf16),
            shape((8, COLS), f32),
            shape((3, PANEL, ORDER), f32),
            shape((16, QC), f32),
            shape((2, KC, KC), f32),
            shape((PANEL, COLS), f32),
        ),
        in_specs=[hbm] * 8,
        out_specs=(vmem,) * 6,
        scratch_shapes=[
            pltpu.VMEM((2, SIDE) + block, bf16),
            pltpu.VMEM((2, SIDE) + block, bf16),
            pltpu.VMEM((2, SIDE - 1) + block, bf16),
            pltpu.VMEM((2, SIDE - 1) + block, bf16),
            pltpu.VMEM((2,) + block, f32),
            pltpu.VMEM((2, SIDE - 1, HALF, COLS), bf16),
            pltpu.VMEM((2, SIDE - 1, HALF, COLS), bf16),
            pltpu.VMEM(grid, bf16),
            pltpu.VMEM((3, PANEL, ORDER), f32),
            pltpu.VMEM((3, PANEL, ORDER), bf16),
            pltpu.VMEM((16, QC), f32),
            pltpu.VMEM((2, KC, KC), f32),
            pltpu.VMEM((QC, QC), bf16),
            pltpu.VMEM((2, KC, KC), bf16),
            pltpu.VMEM((PANEL, COLS), f32),
            pltpu.VMEM((2 * KC, 2 * KC), bf16),
            pltpu.VMEM((128, QC), f32),
            pltpu.VMEM((3, 8, 128), f32),
            pltpu.VMEM((6 * SIDE, 8, 128), f32),
            pltpu.SemaphoreType.DMA((10,)),
            pltpu.SemaphoreType.DMA((33,)),
            pltpu.SemaphoreType.DMA((15,)),
        ],
        compiler_params=pltpu.CompilerParams(
            collective_id=0, has_side_effects=True, vmem_limit_bytes=40 * 1024 * 1024
        ),
    )(
        *(
            pltpu.with_memory_space_constraint(array, pltpu.HBM)
            for array in (
                grads.reshape(grid), left_factor[0], left_root[0], right_q[0], right_kv[0],
                right_q_root[0], right_kv_root[0], moment,
            )
        )
    )
    direction, left_new, rq_new, rkv_new, mom_new = pl.pallas_call(
        finish,
        out_shape=(
            shape((ORDER, COLS), bf16),
            shape((3, PANEL, ORDER), f32),
            shape((16, QC), f32),
            shape((2, KC, KC), f32),
            shape((PANEL, COLS), f32),
        ),
        in_specs=[vmem] * 6,
        out_specs=(hbm,) * 5,
        scratch_shapes=[
            pltpu.VMEM((SIDE, ORDER // SIDE, COLS), bf16),
            pltpu.SemaphoreType.DMA((4 + SIDE,)),
        ],
        compiler_params=pltpu.CompilerParams(vmem_limit_bytes=40 * 1024 * 1024),
    )(gathered, scale_row, left_new, rq_new, rkv_new, mom_new)
    return direction, left_new[None], rq_new[None], rkv_new[None], mom_new


def solution(mesh):
    return jax.shard_map(
        local_step,
        mesh=mesh,
        in_specs=(
            P("dp", None, "mp"),
            P("mp", None, "dp", None),
            P("mp", None, "dp", None),
            P("mp", "dp", None),
            P("mp", None, None, None),
            P("mp", None, None),
            P("mp", None, None, None),
            P("dp", "mp"),
        ),
        out_specs=(
            P(None, "mp"),
            P("mp", None, "dp", None),
            P("mp", "dp", None),
            P("mp", None, None, None),
            P("dp", "mp"),
        ),
        check_vma=False,
    )
```

```python
import jax
import jax.numpy as jnp
from jax import lax
from jax.experimental import pallas as pl
from jax.experimental.pallas import tpu as pltpu
from jax.sharding import PartitionSpec as P

MESH = pl.DeviceIdType.MESH
f32 = jnp.float32
bf16 = jnp.bfloat16

factor_keep = 0.95
factor_add = 0.05
moment_keep = 0.99
moment_add = 0.01
graft_eps = 1e-08
norm_eps = 1e-06

SIDE = 4
HALF = 16
QC = 512
KC = 64
COLS = QC + 2 * KC
ORDER = 1024
PANEL = 32
FLIPS = ((1, 1), (1, 0), (0, 1))


def dot(a, b, ca=1, cb=0):
    return lax.dot_general(a, b, (((ca,), (cb,)), ((), ())), preferred_element_type=f32)


def in_order(ref, cols, lines=range(SIDE)):
    return jnp.concatenate(
        [
            ref[h, (i + 1 - h) % SIDE, (j + 1 - h) % SIDE, k, :, cols]
            for i in lines for j in range(SIDE) for k in range(2) for h in range(2)
        ],
        axis=0,
    )


def kernel(
    g, lf, lr, rq, rkv, rqr, rkvr, mom,
    gathered, scale_row, left_new, rq_new, rkv_new, mom_new,
    own, sib, part, recv1, acc, part2, recv2, total,
    lf_v, lr_v, rq_v, rkv_v, rqr_v, rkvr_v, mom_v,
    diag, slab, norm, norm_in,
    ssem, rsem, lsem,
):
    dp = lax.axis_index("dp")
    z = lax.axis_index("mp")
    core = lax.rem(dp, 2)
    other = 1 - core
    y = lax.rem(dp // 2, SIDE)
    x = dp // (2 * SIDE)
    depth = lax.axis_size("mp")

    def at(i, j, k):
        return ((i * SIDE + j) * 2 + k, z)

    sibling = at(x, y, other)
    halves = range(2)
    u = [lax.rem(x + 1, SIDE), x]
    v = [lax.rem(y + 1, SIDE), y]

    def near(place):
        odd = lax.rem(place, 2)
        return place + 1 - 2 * odd, lax.rem(place + SIDE - 1 + 2 * odd, SIDE)

    def back(h, place):
        return lax.rem(place + SIDE - 1 + h, SIDE)

    def quad(h, kind, k):
        i = (x, back(h, near(u[h])[kind]))
        j = (y, back(h, near(v[h])[kind]))
        return [at(i[a], j[b], k) for a, b in FLIPS]

    small = [quad(h, 0, core) for h in halves]
    large = [quad(h, 1, core) for h in halves]
    crossed = quad(0, 1, other)
    on_z = [(dp, lax.rem(z + k, depth)) for k in range(1, depth)]

    barrier = pltpu.get_barrier_semaphore()
    partners = [sibling] + large[0] + large[1] + crossed + on_z
    for device in partners:
        pl.semaphore_signal(barrier, inc=1, device_id=device, device_id_type=MESH)

    local = []

    def load(src, dst):
        copy = pltpu.make_async_copy(src, dst, lsem.at[len(local)])
        copy.start()
        local.append(copy)
        return copy

    pair_u = [u[h] // 2 for h in halves]
    pair_v = [v[h] // 2 for h in halves]
    lines = [
        [back(h, 2 * (1 - pair_u[h])), back(h, 3 - 2 * pair_u[h]), back(h, 2 * pair_u[h]), back(h, 2 * pair_u[h] + 1)]
        for h in halves
    ]
    mine = {(h, i): load(g.at[lines[h][i], :, core, h], own.at[h, i]) for i in range(SIDE) for h in halves}
    pl.semaphore_wait(barrier, len(partners))

    sends = {}
    arrivals = {}

    def send(src, dst, device, outgoing, incoming):
        i = sends.setdefault(outgoing, len(sends))
        j = arrivals.setdefault(incoming, len(arrivals))
        pltpu.make_async_remote_copy(
            src_ref=src, dst_ref=dst, send_sem=ssem.at[i], recv_sem=rsem.at[j],
            device_id=device, device_id_type=MESH,
        ).start()

    def all_of(ref, outgoing=None, incoming=None):
        copy = pltpu.make_async_remote_copy(
            src_ref=ref, dst_ref=ref,
            send_sem=ssem.at[sends[outgoing] if outgoing else 0],
            recv_sem=rsem.at[arrivals[incoming] if incoming else 0],
            device_id=sibling, device_id_type=MESH,
        )
        if outgoing:
            copy.wait_send()
        else:
            copy.wait_recv()

    for i in range(SIDE):
        for h in halves:
            send(g.at[lines[h][i], :, other, h], sib.at[h, i], sibling, "pair", ("pair", h, i))

    mom_load = load(mom, mom_v)
    lr_load = load(lr, lr_v)
    rqr_load = load(rqr, rqr_v)
    rkvr_load = load(rkvr, rkvr_v)
    rest = [load(lf, lf_v), load(rq, rq_v), load(rkv, rkv_v)]

    def pair_sum(h, a, flip_u, flip_v, b):
        i = a if flip_u else 2 + a
        pair = 1 - pair_v[h] if flip_v else pair_v[h]
        j = back(h, 2 * pair + b)
        return own[h, i, j].astype(f32) + sib[h, i, j].astype(f32)

    for flip_u in (1, 0):
        for h in halves:
            for i in (0, 1) if flip_u else (2, 3):
                mine[h, i].wait()
                all_of(sib.at[h, i], incoming=("pair", h, i))
            for flip_v in (1, 0):
                for a in range(2):
                    for b in range(2):
                        value = pair_sum(h, a, flip_u, flip_v, b)
                        if flip_u or flip_v:
                            part[h, FLIPS.index((flip_u, flip_v)), a, b] = value.astype(bf16)
                        else:
                            acc[h, a, b] = value
                if flip_u or flip_v:
                    i = FLIPS.index((flip_u, flip_v))
                    send(part.at[h, i], recv1.at[h, i], large[h][i], "step1", ("step1", h))

    odd_u = [lax.rem(u[h], 2) for h in halves]
    odd_v = [lax.rem(v[h], 2) for h in halves]

    def quad_sum(h, flip_u, flip_v):
        a = 1 - odd_u[h] if flip_u else odd_u[h]
        b = 1 - odd_v[h] if flip_v else odd_v[h]
        value = acc[h, a, b]
        for i in range(3):
            value = value + recv1[h, i, a, b].astype(f32)
        return value

    kept = []
    for h in halves:
        all_of(recv1.at[h], incoming=("step1", h))
        for i in range(3):
            part2[h, i] = quad_sum(h, *FLIPS[i]).astype(bf16)
            send(part2.at[h, i], recv2.at[h, i], small[h][i], "step2", ("step2", h))
        kept.append(quad_sum(h, 0, 0))
    three = recv2.at[0]

    def across(ref, name, h):
        block = ref.at[h, u[h], v[h], core]
        for i in range(3):
            send(block, block, small[h][i], "across" + name, ("across" + name, h))

    for h in halves:
        value = kept[h]
        all_of(recv2.at[h], incoming=("step2", h))
        for i in range(3):
            value = value + recv2[h, i].astype(f32)
        total[h, u[h], v[h], core] = value.astype(bf16)
        across(total, "0", h)

    def group(ref, h, flip_u, flip_v):
        i = 1 - pair_u[h] if flip_u else pair_u[h]
        j = 1 - pair_v[h] if flip_v else pair_v[h]
        return ref.at[h, pl.ds(2 * i, 2), pl.ds(2 * j, 2), core]

    def gather(ref, name, early, middle, late):
        early()
        for h in halves:
            all_of(three, incoming=("across" + name, h))
            block = group(ref, h, 0, 0)
            for i in range(3):
                send(block, block, large[h][i], "along" + name, ("along" + name, h, i))
        for h in halves:
            block = group(ref, h, 0, 0)
            send(block, block, sibling, "over" + name, "over" + name)
        middle()
        for i in (1, 2, 0):
            for h in halves:
                block = group(ref, h, *FLIPS[i])
                all_of(block, incoming=("along" + name, h, i))
                send(block, block, sibling, "over" + name, "over" + name)
        late()
        all_of(ref.at[:, :, :, other], incoming="over" + name)

    lane = lax.broadcasted_iota(jnp.int32, (1, 2 * KC), 1)
    is_key = lane < KC

    def to_lanes(square):
        column = jnp.sum(square, axis=0, keepdims=True)
        query = column[:, :128]
        for i in range(1, QC // 128):
            query = query + column[:, 128 * i : 128 * (i + 1)]
        return query, column[:, QC:]

    def my_rows():
        return jnp.concatenate([total[h, u[h], v[h], core] for h in halves], axis=0)

    def graft_part():
        mom_load.wait()
        row_grad = my_rows().astype(f32)
        moment_new = moment_keep * mom_v[...] + moment_add * row_grad * row_grad
        mom_new[...] = moment_new
        graft = row_grad / (jnp.sqrt(moment_new) + graft_eps)
        graft_q, graft_kv = to_lanes(jnp.square(graft))
        norm[0] = jnp.zeros((8, 128), f32)
        norm[0, 0:1, :] = graft_q
        norm[0, 1:2, :] = graft_kv

    def diagonal_part():
        rkvr_load.wait()
        row = lax.broadcasted_iota(jnp.int32, (KC, 2 * KC), 0)
        col = lax.broadcasted_iota(jnp.int32, (KC, 2 * KC), 1)
        for i in range(2):
            place = (col == row + i * KC).astype(f32).astype(bf16)
            diag[KC * i : KC * (i + 1), :] = dot(rkvr_v[i], place).astype(bf16)

    def wait_loads():
        lr_load.wait()
        rqr_load.wait()
        for copy in rest:
            copy.wait()

    gather(total, "0", graft_part, diagonal_part, wait_loads)

    def query_grad():
        return in_order(total, slice(0, QC))

    def key_value_grad():
        return in_order(total, slice(QC, COLS))

    proj_q = dot(lr_v[0], query_grad()).astype(bf16)
    both = dot(lr_v[1:3].reshape(2 * PANEL, ORDER), key_value_grad())
    proj_kv = jnp.where(is_key, both[:PANEL], both[PANEL:]).astype(bf16)
    cond_q = dot(proj_q, rqr_v[...])
    cond_kv = dot(proj_kv, diag[...])

    levels = (
        (0, 8, 4 * lax.rem(x, 2) + 2 * lax.rem(y, 2) + core, large[0] + [sibling] + crossed),
        (8, 4, 2 * odd_u[0] + odd_v[0], large[1]),
        (12, depth, z, on_z),
    )

    def norm_send(level):
        start, _, place, devices = levels[level]
        norm_in[start + place] = norm[level]
        for device in devices:
            send(norm.at[level], norm_in.at[start + place], device, "norm", ("norm", level))

    def norm_add(level):
        start, count, _, _ = levels[level]
        all_of(norm_in.at[start : start + count - 1], incoming=("norm", level))
        value = norm_in[start]
        for i in range(1, count):
            value = value + norm_in[start + i]
        return value

    def norm_step(level):
        norm[level] = norm_add(level - 1)
        norm_send(level)

    square = jnp.square(jnp.concatenate([cond_q, cond_kv], axis=1))
    cond_lanes_q, cond_lanes_kv = to_lanes(square)
    norm[0, 2:3, :] = cond_lanes_q
    norm[0, 3:4, :] = cond_lanes_kv
    norm_send(0)
    for h in halves:
        rows = slice(HALF * h, HALF * (h + 1))
        gathered[h, u[h], v[h], core, :, :QC] = cond_q[rows].astype(bf16)
        gathered[h, u[h], v[h], core, :, QC:] = cond_kv[rows].astype(bf16)
        across(gathered, "1", h)

    def left_part():
        owned = my_rows()
        owned_kv = owned[:, QC:].astype(f32)
        split = jnp.concatenate(
            [jnp.where(is_key, owned_kv, 0.0), jnp.where(is_key, 0.0, owned_kv)], axis=0
        ).astype(bf16)
        both = dot(split, key_value_grad(), 1, 1)
        left_new[1] = factor_keep * lf_v[1] + factor_add * both[:PANEL]
        left_new[2] = factor_keep * lf_v[2] + factor_add * both[PANEL:]
        left_new[0] = factor_keep * lf_v[0] + factor_add * dot(owned[:, :QC], query_grad(), 1, 1)

    def right_part():
        columns = pl.ds(pl.multiple_of(x * 128, 128), 128)
        slab[...] = dot(
            total[..., columns].reshape(ORDER, 128), total[..., :QC].reshape(ORDER, QC), 0, 0
        )
        mine_q = pl.ds(pl.multiple_of(lax.rem(dp, 2 * SIDE) * 16, 16), 16)
        rq_new[...] = factor_keep * rq_v[...] + factor_add * slab[mine_q, :]
        key_value = total[..., QC:].reshape(ORDER, 2 * KC)
        square = dot(key_value, key_value, 0, 0)
        rkv_new[0] = factor_keep * rkv_v[0] + factor_add * square[:KC, :KC]
        moved = pltpu.roll(square, KC, 1)
        rkv_new[1] = factor_keep * rkv_v[1] + factor_add * moved[KC:, :KC]

    def early_part():
        left_part()
        norm_step(1)
        right_part()
        norm_step(2)

    def wait_rest():
        pass

    def scale_part():
        sums = norm_add(2)

        def whole(row_index, mask):
            values = sums[row_index : row_index + 1, :]
            if mask is not None:
                values = jnp.where(mask, values, 0.0)
            return jnp.sum(values, axis=1, keepdims=True)

        def scale(graft_sq, shampoo_sq):
            return jnp.sqrt(graft_sq / (shampoo_sq + norm_eps))

        scale_q = scale(whole(0, None), whole(2, None))
        scale_k = scale(whole(1, is_key), whole(3, is_key))
        scale_v = scale(whole(1, lane >= KC), whole(3, lane >= KC))
        scale_row[:, :QC] = jnp.broadcast_to(scale_q, (8, QC))
        scale_row[:, QC:] = jnp.broadcast_to(jnp.where(is_key, scale_k, scale_v), (8, 2 * KC))

    gather(gathered, "1", early_part, wait_rest, scale_part)

    all_of(sib, outgoing="pair")
    all_of(recv1, outgoing="step1")
    all_of(recv2, outgoing="step2")
    for name, ref in (("0", total), ("1", gathered)):
        all_of(recv2, outgoing="across" + name)
        all_of(recv1, outgoing="along" + name)
        all_of(ref.at[:, :, :, core], outgoing="over" + name)
    all_of(norm_in.at[: 7 + 3 + depth - 1], outgoing="norm")
    assert len(sends) == ssem.shape[0] and len(arrivals) == rsem.shape[0]


def finish(gathered, scale_row, left, rq, rkv, mom, direction, left_out, rq_out, rkv_out, mom_out, rows, sem):
    copies = []

    def store(src, dst):
        copy = pltpu.make_async_copy(src, dst, sem.at[len(copies)])
        copy.start()
        copies.append(copy)

    for src, dst in ((left, left_out), (mom, mom_out), (rq, rq_out), (rkv, rkv_out)):
        store(src, dst)
    height = ORDER // SIDE
    scale = scale_row[0:1, :]
    for i in range(SIDE):
        rows[i] = (in_order(gathered, slice(0, COLS), (i,)).astype(f32) * scale).astype(bf16)
        store(rows.at[i], direction.at[pl.ds(i * height, height)])
    for copy in copies:
        copy.wait()


def local_step(grads, left_factor, left_root, right_q, right_kv, right_q_root, right_kv_root, moment):
    grid = (SIDE, SIDE, 2, 2, HALF, COLS)
    by_half = (2, SIDE, SIDE, 2, HALF, COLS)
    depth = lax.axis_size("mp")
    quad_block = (2, 2, HALF, COLS)
    block = (SIDE, HALF, COLS)
    hbm = pl.BlockSpec(memory_space=pltpu.HBM)
    vmem = pl.BlockSpec(memory_space=pltpu.VMEM)
    shape = jax.ShapeDtypeStruct
    gathered, scale_row, left_new, rq_new, rkv_new, mom_new = pl.pallas_call(
        kernel,
        out_shape=(
            shape(by_half, bf16),
            shape((8, COLS), f32),
            shape((3, PANEL, ORDER), f32),
            shape((16, QC), f32),
            shape((2, KC, KC), f32),
            shape((PANEL, COLS), f32),
        ),
        in_specs=[hbm] * 8,
        out_specs=(vmem,) * 6,
        scratch_shapes=[
            pltpu.VMEM((2, SIDE) + block, bf16),
            pltpu.VMEM((2, SIDE) + block, bf16),
            pltpu.VMEM((2, 3) + quad_block, bf16),
            pltpu.VMEM((2, 3) + quad_block, bf16),
            pltpu.VMEM((2,) + quad_block, f32),
            pltpu.VMEM((2, SIDE - 1, HALF, COLS), bf16),
            pltpu.VMEM((2, SIDE - 1, HALF, COLS), bf16),
            pltpu.VMEM(by_half, bf16),
            pltpu.VMEM((3, PANEL, ORDER), f32),
            pltpu.VMEM((3, PANEL, ORDER), bf16),
            pltpu.VMEM((16, QC), f32),
            pltpu.VMEM((2, KC, KC), f32),
            pltpu.VMEM((QC, QC), bf16),
            pltpu.VMEM((2, KC, KC), bf16),
            pltpu.VMEM((PANEL, COLS), f32),
            pltpu.VMEM((2 * KC, 2 * KC), bf16),
            pltpu.VMEM((128, QC), f32),
            pltpu.VMEM((3, 8, 128), f32),
            pltpu.VMEM((12 + depth, 8, 128), f32),
            pltpu.SemaphoreType.DMA((10,)),
            pltpu.SemaphoreType.DMA((33,)),
            pltpu.SemaphoreType.DMA((15,)),
        ],
        compiler_params=pltpu.CompilerParams(
            collective_id=0, has_side_effects=True, vmem_limit_bytes=40 * 1024 * 1024
        ),
    )(
        *(
            pltpu.with_memory_space_constraint(array, pltpu.HBM)
            for array in (
                grads.reshape(grid), left_factor[0], left_root[0], right_q[0], right_kv[0],
                right_q_root[0], right_kv_root[0], moment,
            )
        )
    )
    direction, left_new, rq_new, rkv_new, mom_new = pl.pallas_call(
        finish,
        out_shape=(
            shape((ORDER, COLS), bf16),
            shape((3, PANEL, ORDER), f32),
            shape((16, QC), f32),
            shape((2, KC, KC), f32),
            shape((PANEL, COLS), f32),
        ),
        in_specs=[vmem] * 6,
        out_specs=(hbm,) * 5,
        scratch_shapes=[
            pltpu.VMEM((SIDE, ORDER // SIDE, COLS), bf16),
            pltpu.SemaphoreType.DMA((4 + SIDE,)),
        ],
        compiler_params=pltpu.CompilerParams(vmem_limit_bytes=40 * 1024 * 1024),
    )(gathered, scale_row, left_new, rq_new, rkv_new, mom_new)
    return direction, left_new[None], rq_new[None], rkv_new[None], mom_new


def solution(mesh):
    return jax.shard_map(
        local_step,
        mesh=mesh,
        in_specs=(
            P("dp", None, "mp"),
            P("mp", None, "dp", None),
            P("mp", None, "dp", None),
            P("mp", "dp", None),
            P("mp", None, None, None),
            P("mp", None, None),
            P("mp", None, None, None),
            P("dp", "mp"),
        ),
        out_specs=(
            P(None, "mp"),
            P("mp", None, "dp", None),
            P("mp", "dp", None),
            P("mp", None, None, None),
            P("dp", "mp"),
        ),
        check_vma=False,
    )
```

```python
import jax
import jax.numpy as jnp
from jax import lax
from jax.experimental import pallas as pl
from jax.experimental.pallas import tpu as pltpu
from jax.sharding import PartitionSpec as P

MESH = pl.DeviceIdType.MESH
f32 = jnp.float32
bf16 = jnp.bfloat16

factor_keep = 0.95
factor_add = 0.05
moment_keep = 0.99
moment_add = 0.01
graft_eps = 1e-08
norm_eps = 1e-06

SIDE = 4
HALF = 16
QC = 512
KC = 64
COLS = QC + 2 * KC
ORDER = 1024
PANEL = 32
FLIPS = ((1, 1), (1, 0), (0, 1))


def dot(a, b, ca=1, cb=0):
    return lax.dot_general(a, b, (((ca,), (cb,)), ((), ())), preferred_element_type=f32)


def in_order(ref, cols, lines=range(SIDE)):
    return jnp.concatenate(
        [
            ref[h, (i + 1 - h) % SIDE, (j + 1 - h) % SIDE, k, :, cols]
            for i in lines for j in range(SIDE) for k in range(2) for h in range(2)
        ],
        axis=0,
    )


def kernel(
    g, lf, lr, rq, rkv, rqr, rkvr, mom,
    gathered, scale_row, left_new, rq_new, rkv_new, mom_new,
    own, sib, part, recv1, acc, part2, recv2, total,
    lf_v, lr_v, rq_v, rkv_v, rqr_v, rkvr_v, mom_v,
    roots_by, diag, slab, norm, norm_in,
    ssem, rsem, lsem, known,
):
    dp = lax.axis_index("dp")
    z = lax.axis_index("mp")
    core = lax.rem(dp, 2)
    other = 1 - core
    y = lax.rem(dp // 2, SIDE)
    x = dp // (2 * SIDE)
    depth = lax.axis_size("mp")

    def at(i, j, k):
        return ((i * SIDE + j) * 2 + k, z)

    sibling = at(x, y, other)
    halves = range(2)
    u = [lax.rem(x + 1, SIDE), x]
    v = [lax.rem(y + 1, SIDE), y]

    def near(place):
        odd = lax.rem(place, 2)
        return place + 1 - 2 * odd, lax.rem(place + SIDE - 1 + 2 * odd, SIDE)

    def back(h, place):
        return lax.rem(place + SIDE - 1 + h, SIDE)

    def quad(h, kind, k):
        i = (x, back(h, near(u[h])[kind]))
        j = (y, back(h, near(v[h])[kind]))
        return [at(i[a], j[b], k) for a, b in FLIPS]

    small = [quad(h, 0, core) for h in halves]
    large = [quad(h, 1, core) for h in halves]
    crossed = quad(0, 1, other)
    far_first = sorted(range(1, depth), key=lambda k: -min(k, depth - k))
    on_z = [(dp, lax.rem(z + k, depth)) for k in far_first]

    def beside(k):
        return [(dp, lax.rem(z + k, depth)), (dp, lax.rem(z + depth - k, depth))]

    barrier = pltpu.get_barrier_semaphore()
    partners = [sibling] + large[0] + large[1] + crossed + beside(1)
    for device in partners:
        pl.semaphore_signal(barrier, inc=1, device_id=device, device_id_type=MESH)

    local = []

    def load(src, dst):
        copy = pltpu.make_async_copy(src, dst, lsem.at[len(local)])
        copy.start()
        local.append(copy)
        return copy

    pair_u = [u[h] // 2 for h in halves]
    pair_v = [v[h] // 2 for h in halves]
    lines = [
        [back(h, 2 * (1 - pair_u[h])), back(h, 3 - 2 * pair_u[h]), back(h, 2 * pair_u[h]), back(h, 2 * pair_u[h] + 1)]
        for h in halves
    ]
    mine = {(h, i): load(g.at[lines[h][i], :, core, h], own.at[h, i]) for i in range(SIDE) for h in halves}
    pl.semaphore_wait(barrier, len(partners))

    def tell(i):
        for device in beside(2**i):
            pl.semaphore_signal(known.at[i], inc=1, device_id=device, device_id_type=MESH)

    def learn(i):
        pl.semaphore_wait(known.at[i], 2)

    tell(0)

    sends = {}
    arrivals = {}

    def send(src, dst, device, outgoing, incoming):
        i = sends.setdefault(outgoing, len(sends))
        j = arrivals.setdefault(incoming, len(arrivals))
        pltpu.make_async_remote_copy(
            src_ref=src, dst_ref=dst, send_sem=ssem.at[i], recv_sem=rsem.at[j],
            device_id=device, device_id_type=MESH,
        ).start()

    def all_of(ref, outgoing=None, incoming=None):
        copy = pltpu.make_async_remote_copy(
            src_ref=ref, dst_ref=ref,
            send_sem=ssem.at[sends[outgoing] if outgoing else 0],
            recv_sem=rsem.at[arrivals[incoming] if incoming else 0],
            device_id=sibling, device_id_type=MESH,
        )
        if outgoing:
            copy.wait_send()
        else:
            copy.wait_recv()

    for i in range(SIDE):
        for h in halves:
            send(g.at[lines[h][i], :, other, h], sib.at[h, i], sibling, "pair", ("pair", h, i))

    mom_load = load(mom, mom_v)
    lr_load = load(lr, lr_v)
    rqr_load = load(rqr, rqr_v)
    rkvr_load = load(rkvr, rkvr_v)
    rest = [load(lf, lf_v), load(rq, rq_v), load(rkv, rkv_v)]

    def pair_sum(h, a, flip_u, flip_v, b):
        i = a if flip_u else 2 + a
        pair = 1 - pair_v[h] if flip_v else pair_v[h]
        j = back(h, 2 * pair + b)
        return own[h, i, j].astype(f32) + sib[h, i, j].astype(f32)

    for flip_u in (1, 0):
        for h in halves:
            for i in (0, 1) if flip_u else (2, 3):
                mine[h, i].wait()
                all_of(sib.at[h, i], incoming=("pair", h, i))
            for flip_v in (1, 0):
                for a in range(2):
                    for b in range(2):
                        value = pair_sum(h, a, flip_u, flip_v, b)
                        if flip_u or flip_v:
                            part[h, FLIPS.index((flip_u, flip_v)), a, b] = value.astype(bf16)
                        else:
                            acc[h, a, b] = value
                if flip_u or flip_v:
                    i = FLIPS.index((flip_u, flip_v))
                    send(part.at[h, i], recv1.at[h, i], large[h][i], "step1", ("step1", h))

    learn(0)
    tell(1)

    lr_load.wait()
    roots = lr_v[...].reshape(3 * PANEL, ORDER)
    column = lax.broadcasted_iota(jnp.int32, (1, ORDER // 2), 1)
    half_of = column >> 8
    u_of = ((column >> 6) + SIDE - 1 + half_of) & (SIDE - 1)
    v_of = ((column >> 4) + SIDE - 1 + half_of) & (SIDE - 1)
    wanted = u_of * 256 + v_of * 64 + half_of * HALF + (column & (HALF - 1))
    row_of = lax.broadcasted_iota(jnp.int32, (ORDER, ORDER // 2), 0)
    for i, parity in enumerate((core, other)):
        chosen = jnp.where(row_of == wanted + parity * PANEL, 1.0, 0.0).astype(bf16)
        roots_by[i] = dot(roots, chosen).astype(bf16)

    odd_u = [lax.rem(u[h], 2) for h in halves]
    odd_v = [lax.rem(v[h], 2) for h in halves]

    def quad_sum(h, flip_u, flip_v):
        a = 1 - odd_u[h] if flip_u else odd_u[h]
        b = 1 - odd_v[h] if flip_v else odd_v[h]
        value = acc[h, a, b]
        for i in range(3):
            value = value + recv1[h, i, a, b].astype(f32)
        return value

    kept = []
    for h in halves:
        all_of(recv1.at[h], incoming=("step1", h))
        for i in range(3):
            part2[h, i] = quad_sum(h, *FLIPS[i]).astype(bf16)
            send(part2.at[h, i], recv2.at[h, i], small[h][i], "step2", ("step2", h))
        kept.append(quad_sum(h, 0, 0))
    three = recv2.at[0]

    def across(ref, name, h):
        block = ref.at[h, u[h], v[h], core]
        for i in range(3):
            send(block, block, small[h][i], "across" + name, ("across" + name, h))

    for h in halves:
        value = kept[h]
        all_of(recv2.at[h], incoming=("step2", h))
        for i in range(3):
            value = value + recv2[h, i].astype(f32)
        total[h, u[h], v[h], core] = value.astype(bf16)
        across(total, "0", h)

    def group(ref, h, flip_u, flip_v):
        i = 1 - pair_u[h] if flip_u else pair_u[h]
        j = 1 - pair_v[h] if flip_v else pair_v[h]
        return ref.at[h, pl.ds(2 * i, 2), pl.ds(2 * j, 2), core]

    def gather(ref, name, early, middle, late):
        early()
        for h in halves:
            all_of(three, incoming=("across" + name, h))
            block = group(ref, h, 0, 0)
            for i in range(3):
                send(block, block, large[h][i], "along" + name, ("along" + name, h, i))
        for h in halves:
            block = group(ref, h, 0, 0)
            send(block, block, sibling, "over" + name, "over" + name)
        middle()
        for i in (1, 2, 0):
            for h in halves:
                block = group(ref, h, *FLIPS[i])
                all_of(block, incoming=("along" + name, h, i))
                send(block, block, sibling, "over" + name, "over" + name)
        late()
        all_of(ref.at[:, :, :, other], incoming="over" + name)

    lane = lax.broadcasted_iota(jnp.int32, (1, 2 * KC), 1)
    is_key = lane < KC

    def to_lanes(square):
        column = jnp.sum(square, axis=0, keepdims=True)
        query = column[:, :128]
        for i in range(1, QC // 128):
            query = query + column[:, 128 * i : 128 * (i + 1)]
        return query, column[:, QC:]

    def my_rows():
        return jnp.concatenate([total[h, u[h], v[h], core] for h in halves], axis=0)

    def graft_part():
        mom_load.wait()
        row_grad = my_rows().astype(f32)
        moment_new = moment_keep * mom_v[...] + moment_add * row_grad * row_grad
        mom_new[...] = moment_new
        graft = row_grad / (jnp.sqrt(moment_new) + graft_eps)
        graft_q, graft_kv = to_lanes(jnp.square(graft))
        norm[0] = jnp.zeros((8, 128), f32)
        norm[0, 0:1, :] = graft_q
        norm[0, 1:2, :] = graft_kv

    def diagonal_part():
        rkvr_load.wait()
        row = lax.broadcasted_iota(jnp.int32, (KC, 2 * KC), 0)
        col = lax.broadcasted_iota(jnp.int32, (KC, 2 * KC), 1)
        for i in range(2):
            place = (col == row + i * KC).astype(f32).astype(bf16)
            diag[KC * i : KC * (i + 1), :] = dot(rkvr_v[i], place).astype(bf16)

    saved = []

    def project(i, parity):
        rows_q = total[:, :, :, parity, :, :QC].reshape(ORDER // 2, QC)
        rows_kv = total[:, :, :, parity, :, QC:].reshape(ORDER // 2, 2 * KC)
        return dot(roots_by[i, :PANEL], rows_q), dot(roots_by[i, PANEL:], rows_kv)

    def wait_loads():
        rqr_load.wait()
        for copy in rest:
            copy.wait()
        saved.append(project(0, core))

    def middle_part():
        diagonal_part()
        learn(1)
        tell(2)

    gather(total, "0", graft_part, middle_part, wait_loads)

    def query_grad():
        return in_order(total, slice(0, QC))

    def key_value_grad():
        return in_order(total, slice(QC, COLS))

    saved.append(project(1, other))
    proj_q = (saved[0][0] + saved[1][0]).astype(bf16)
    both = saved[0][1] + saved[1][1]
    proj_kv = jnp.where(is_key, both[:PANEL], both[PANEL:]).astype(bf16)
    cond_q = dot(proj_q, rqr_v[...])
    cond_kv = dot(proj_kv, diag[...])

    levels = (
        (0, 8, 4 * lax.rem(x, 2) + 2 * lax.rem(y, 2) + core, large[0] + [sibling] + crossed),
        (8, 4, 2 * odd_u[0] + odd_v[0], large[1]),
        (12, depth, z, on_z),
    )

    def norm_send(level):
        start, _, place, devices = levels[level]
        norm_in[start + place] = norm[level]
        for device in devices:
            send(norm.at[level], norm_in.at[start + place], device, "norm", ("norm", level))

    def norm_add(level):
        start, count, _, _ = levels[level]
        all_of(norm_in.at[start : start + count - 1], incoming=("norm", level))
        value = norm_in[start]
        for i in range(1, count):
            value = value + norm_in[start + i]
        return value

    def norm_step(level):
        norm[level] = norm_add(level - 1)
        norm_send(level)

    square = jnp.square(jnp.concatenate([cond_q, cond_kv], axis=1))
    cond_lanes_q, cond_lanes_kv = to_lanes(square)
    norm[0, 2:3, :] = cond_lanes_q
    norm[0, 3:4, :] = cond_lanes_kv
    norm_send(0)
    for h in halves:
        rows = slice(HALF * h, HALF * (h + 1))
        gathered[h, u[h], v[h], core, :, :QC] = cond_q[rows].astype(bf16)
        gathered[h, u[h], v[h], core, :, QC:] = cond_kv[rows].astype(bf16)
        across(gathered, "1", h)

    def left_part():
        owned = my_rows()
        owned_kv = owned[:, QC:].astype(f32)
        split = jnp.concatenate(
            [jnp.where(is_key, owned_kv, 0.0), jnp.where(is_key, 0.0, owned_kv)], axis=0
        ).astype(bf16)
        both = dot(split, key_value_grad(), 1, 1)
        left_new[1] = factor_keep * lf_v[1] + factor_add * both[:PANEL]
        left_new[2] = factor_keep * lf_v[2] + factor_add * both[PANEL:]
        left_new[0] = factor_keep * lf_v[0] + factor_add * dot(owned[:, :QC], query_grad(), 1, 1)

    def right_part():
        columns = pl.ds(pl.multiple_of(x * 128, 128), 128)
        slab[...] = dot(
            total[..., columns].reshape(ORDER, 128), total[..., :QC].reshape(ORDER, QC), 0, 0
        )
        mine_q = pl.ds(pl.multiple_of(lax.rem(dp, 2 * SIDE) * 16, 16), 16)
        rq_new[...] = factor_keep * rq_v[...] + factor_add * slab[mine_q, :]
        key_value = total[..., QC:].reshape(ORDER, 2 * KC)
        square = dot(key_value, key_value, 0, 0)
        rkv_new[0] = factor_keep * rkv_v[0] + factor_add * square[:KC, :KC]
        moved = pltpu.roll(square, KC, 1)
        rkv_new[1] = factor_keep * rkv_v[1] + factor_add * moved[KC:, :KC]

    def early_part():
        left_part()
        norm_step(1)
        right_part()
        learn(2)
        norm_step(2)

    def wait_rest():
        pass

    def scale_part():
        sums = norm_add(2)

        def whole(row_index, mask):
            values = sums[row_index : row_index + 1, :]
            if mask is not None:
                values = jnp.where(mask, values, 0.0)
            return jnp.sum(values, axis=1, keepdims=True)

        def scale(graft_sq, shampoo_sq):
            return jnp.sqrt(graft_sq / (shampoo_sq + norm_eps))

        scale_q = scale(whole(0, None), whole(2, None))
        scale_k = scale(whole(1, is_key), whole(3, is_key))
        scale_v = scale(whole(1, lane >= KC), whole(3, lane >= KC))
        scale_row[:, :QC] = jnp.broadcast_to(scale_q, (8, QC))
        scale_row[:, QC:] = jnp.broadcast_to(jnp.where(is_key, scale_k, scale_v), (8, 2 * KC))

    gather(gathered, "1", early_part, wait_rest, scale_part)

    all_of(sib, outgoing="pair")
    all_of(recv1, outgoing="step1")
    all_of(recv2, outgoing="step2")
    for name, ref in (("0", total), ("1", gathered)):
        all_of(recv2, outgoing="across" + name)
        all_of(recv1, outgoing="along" + name)
        all_of(ref.at[:, :, :, core], outgoing="over" + name)
    all_of(norm_in.at[: 7 + 3 + depth - 1], outgoing="norm")
    assert len(sends) == ssem.shape[0] and len(arrivals) == rsem.shape[0]


def finish(gathered, scale_row, left, rq, rkv, mom, direction, left_out, rq_out, rkv_out, mom_out, rows, sem):
    copies = []

    def store(src, dst):
        copy = pltpu.make_async_copy(src, dst, sem.at[len(copies)])
        copy.start()
        copies.append(copy)

    for src, dst in ((left, left_out), (mom, mom_out), (rq, rq_out), (rkv, rkv_out)):
        store(src, dst)
    height = ORDER // SIDE
    scale = scale_row[0:1, :]
    for i in range(SIDE):
        rows[i] = (in_order(gathered, slice(0, COLS), (i,)).astype(f32) * scale).astype(bf16)
        store(rows.at[i], direction.at[pl.ds(i * height, height)])
    for copy in copies:
        copy.wait()


def local_step(grads, left_factor, left_root, right_q, right_kv, right_q_root, right_kv_root, moment):
    grid = (SIDE, SIDE, 2, 2, HALF, COLS)
    by_half = (2, SIDE, SIDE, 2, HALF, COLS)
    depth = lax.axis_size("mp")
    quad_block = (2, 2, HALF, COLS)
    block = (SIDE, HALF, COLS)
    hbm = pl.BlockSpec(memory_space=pltpu.HBM)
    vmem = pl.BlockSpec(memory_space=pltpu.VMEM)
    shape = jax.ShapeDtypeStruct
    gathered, scale_row, left_new, rq_new, rkv_new, mom_new = pl.pallas_call(
        kernel,
        out_shape=(
            shape(by_half, bf16),
            shape((8, COLS), f32),
            shape((3, PANEL, ORDER), f32),
            shape((16, QC), f32),
            shape((2, KC, KC), f32),
            shape((PANEL, COLS), f32),
        ),
        in_specs=[hbm] * 8,
        out_specs=(vmem,) * 6,
        scratch_shapes=[
            pltpu.VMEM((2, SIDE) + block, bf16),
            pltpu.VMEM((2, SIDE) + block, bf16),
            pltpu.VMEM((2, 3) + quad_block, bf16),
            pltpu.VMEM((2, 3) + quad_block, bf16),
            pltpu.VMEM((2,) + quad_block, f32),
            pltpu.VMEM((2, SIDE - 1, HALF, COLS), bf16),
            pltpu.VMEM((2, SIDE - 1, HALF, COLS), bf16),
            pltpu.VMEM(by_half, bf16),
            pltpu.VMEM((3, PANEL, ORDER), f32),
            pltpu.VMEM((3, PANEL, ORDER), bf16),
            pltpu.VMEM((16, QC), f32),
            pltpu.VMEM((2, KC, KC), f32),
            pltpu.VMEM((QC, QC), bf16),
            pltpu.VMEM((2, KC, KC), bf16),
            pltpu.VMEM((PANEL, COLS), f32),
            pltpu.VMEM((2, 3 * PANEL, ORDER // 2), bf16),
            pltpu.VMEM((2 * KC, 2 * KC), bf16),
            pltpu.VMEM((128, QC), f32),
            pltpu.VMEM((3, 8, 128), f32),
            pltpu.VMEM((12 + depth, 8, 128), f32),
            pltpu.SemaphoreType.DMA((10,)),
            pltpu.SemaphoreType.DMA((33,)),
            pltpu.SemaphoreType.DMA((15,)),
            pltpu.SemaphoreType.REGULAR((3,)),
        ],
        compiler_params=pltpu.CompilerParams(
            collective_id=0, has_side_effects=True, vmem_limit_bytes=40 * 1024 * 1024
        ),
    )(
        *(
            pltpu.with_memory_space_constraint(array, pltpu.HBM)
            for array in (
                grads.reshape(grid), left_factor[0], left_root[0], right_q[0], right_kv[0],
                right_q_root[0], right_kv_root[0], moment,
            )
        )
    )
    direction, left_new, rq_new, rkv_new, mom_new = pl.pallas_call(
        finish,
        out_shape=(
            shape((ORDER, COLS), bf16),
            shape((3, PANEL, ORDER), f32),
            shape((16, QC), f32),
            shape((2, KC, KC), f32),
            shape((PANEL, COLS), f32),
        ),
        in_specs=[vmem] * 6,
        out_specs=(hbm,) * 5,
        scratch_shapes=[
            pltpu.VMEM((SIDE, ORDER // SIDE, COLS), bf16),
            pltpu.SemaphoreType.DMA((4 + SIDE,)),
        ],
        compiler_params=pltpu.CompilerParams(vmem_limit_bytes=40 * 1024 * 1024),
    )(gathered, scale_row, left_new, rq_new, rkv_new, mom_new)
    return direction, left_new[None], rq_new[None], rkv_new[None], mom_new


def solution(mesh):
    return jax.shard_map(
        local_step,
        mesh=mesh,
        in_specs=(
            P("dp", None, "mp"),
            P("mp", None, "dp", None),
            P("mp", None, "dp", None),
            P("mp", "dp", None),
            P("mp", None, None, None),
            P("mp", None, None),
            P("mp", None, None, None),
            P("dp", "mp"),
        ),
        out_specs=(
            P(None, "mp"),
            P("mp", None, "dp", None),
            P("mp", "dp", None),
            P("mp", None, None, None),
            P("dp", "mp"),
        ),
        check_vma=False,
    )
```

```python
import jax
import jax.numpy as jnp
from jax import lax
from jax.experimental import pallas as pl
from jax.experimental.pallas import tpu as pltpu
from jax.sharding import PartitionSpec as P

MESH = pl.DeviceIdType.MESH
f32 = jnp.float32
bf16 = jnp.bfloat16

factor_keep = 0.95
factor_add = 0.05
moment_keep = 0.99
moment_add = 0.01
graft_eps = 1e-08
norm_eps = 1e-06

SIDE = 4
HALF = 16
QC = 512
KC = 64
COLS = QC + 2 * KC
ORDER = 1024
PANEL = 32
FLIPS = ((1, 1), (1, 0), (0, 1))


def dot(a, b, ca=1, cb=0):
    return lax.dot_general(a, b, (((ca,), (cb,)), ((), ())), preferred_element_type=f32)


def in_order(ref, cols, lines=range(SIDE)):
    return jnp.concatenate(
        [
            ref[h, (i + 1 - h) % SIDE, (j + 1 - h) % SIDE, k, :, cols]
            for i in lines for j in range(SIDE) for k in range(2) for h in range(2)
        ],
        axis=0,
    )


def kernel(
    g, lf, lr, rq, rkv, rqr, rkvr, mom,
    gathered, scale_row, left_new, rq_new, rkv_new, mom_new,
    own, sib, part, recv1, acc, shares, total,
    lf_v, lr_v, rq_v, rkv_v, rqr_v, rkvr_v, mom_v,
    roots_by, diag, slab, norm, norm_in,
    ssem, rsem, lsem, known,
):
    dp = lax.axis_index("dp")
    z = lax.axis_index("mp")
    core = lax.rem(dp, 2)
    other = 1 - core
    y = lax.rem(dp // 2, SIDE)
    x = dp // (2 * SIDE)
    depth = lax.axis_size("mp")

    def at(i, j, k):
        return ((i * SIDE + j) * 2 + k, z)

    sibling = at(x, y, other)
    halves = range(2)
    u = [lax.rem(x + 1, SIDE), x]
    v = [lax.rem(y + 1, SIDE), y]

    def near(place):
        odd = lax.rem(place, 2)
        return place + 1 - 2 * odd, lax.rem(place + SIDE - 1 + 2 * odd, SIDE)

    def back(h, place):
        return lax.rem(place + SIDE - 1 + h, SIDE)

    def quad(h, kind, k):
        i = (x, back(h, near(u[h])[kind]))
        j = (y, back(h, near(v[h])[kind]))
        return [at(i[a], j[b], k) for a, b in FLIPS]

    small = [quad(h, 0, core) for h in halves]
    large = [quad(h, 1, core) for h in halves]
    crossed = quad(0, 1, other)
    far_first = sorted(range(1, depth), key=lambda k: -min(k, depth - k))
    on_z = [(dp, lax.rem(z + k, depth)) for k in far_first]

    def beside(k):
        return [(dp, lax.rem(z + k, depth)), (dp, lax.rem(z + depth - k, depth))]

    barrier = pltpu.get_barrier_semaphore()
    partners = [sibling] + large[0] + large[1] + crossed + beside(1)
    for device in partners:
        pl.semaphore_signal(barrier, inc=1, device_id=device, device_id_type=MESH)

    local = []

    def load(src, dst):
        copy = pltpu.make_async_copy(src, dst, lsem.at[len(local)])
        copy.start()
        local.append(copy)
        return copy

    pair_u = [u[h] // 2 for h in halves]
    pair_v = [v[h] // 2 for h in halves]
    lines = [
        [back(h, 2 * (1 - pair_u[h])), back(h, 3 - 2 * pair_u[h]), back(h, 2 * pair_u[h]), back(h, 2 * pair_u[h] + 1)]
        for h in halves
    ]
    mine = {(h, i): load(g.at[lines[h][i], :, core, h], own.at[h, i]) for i in range(SIDE) for h in halves}
    pl.semaphore_wait(barrier, len(partners))

    def tell(i):
        for device in beside(2**i):
            pl.semaphore_signal(known.at[i], inc=1, device_id=device, device_id_type=MESH)

    def learn(i):
        pl.semaphore_wait(known.at[i], 2)

    tell(0)

    sends = {}
    arrivals = {}

    def send(src, dst, device, outgoing, incoming):
        i = sends.setdefault(outgoing, len(sends))
        j = arrivals.setdefault(incoming, len(arrivals))
        pltpu.make_async_remote_copy(
            src_ref=src, dst_ref=dst, send_sem=ssem.at[i], recv_sem=rsem.at[j],
            device_id=device, device_id_type=MESH,
        ).start()

    def all_of(ref, outgoing=None, incoming=None):
        copy = pltpu.make_async_remote_copy(
            src_ref=ref, dst_ref=ref,
            send_sem=ssem.at[sends[outgoing] if outgoing else 0],
            recv_sem=rsem.at[arrivals[incoming] if incoming else 0],
            device_id=sibling, device_id_type=MESH,
        )
        if outgoing:
            copy.wait_send()
        else:
            copy.wait_recv()

    for i in range(SIDE):
        for h in halves:
            send(g.at[lines[h][i], :, other, h], sib.at[h, i], sibling, "pair", ("pair", h, i))

    mom_load = load(mom, mom_v)
    lr_load = load(lr, lr_v)
    rqr_load = load(rqr, rqr_v)
    rkvr_load = load(rkvr, rkvr_v)
    rest = [load(lf, lf_v), load(rq, rq_v), load(rkv, rkv_v)]

    def pair_sum(h, a, flip_u, flip_v, b):
        i = a if flip_u else 2 + a
        pair = 1 - pair_v[h] if flip_v else pair_v[h]
        j = back(h, 2 * pair + b)
        return own[h, i, j].astype(f32) + sib[h, i, j].astype(f32)

    for flip_u in (1, 0):
        for h in halves:
            for i in (0, 1) if flip_u else (2, 3):
                mine[h, i].wait()
                all_of(sib.at[h, i], incoming=("pair", h, i))
            for flip_v in (1, 0):
                for a in range(2):
                    for b in range(2):
                        value = pair_sum(h, a, flip_u, flip_v, b)
                        if flip_u or flip_v:
                            part[h, FLIPS.index((flip_u, flip_v)), a, b] = value.astype(bf16)
                        else:
                            acc[h, a, b] = value
                if flip_u or flip_v:
                    i = FLIPS.index((flip_u, flip_v))
                    send(part.at[h, i], recv1.at[h, i], large[h][i], "step1", ("step1", h))

    learn(0)
    tell(1)

    lr_load.wait()
    roots = lr_v[...].reshape(3 * PANEL, ORDER)
    column = lax.broadcasted_iota(jnp.int32, (1, ORDER // 2), 1)
    half_of = column >> 8
    u_of = ((column >> 6) + SIDE - 1 + half_of) & (SIDE - 1)
    v_of = ((column >> 4) + SIDE - 1 + half_of) & (SIDE - 1)
    wanted = u_of * 256 + v_of * 64 + half_of * HALF + (column & (HALF - 1))
    row_of = lax.broadcasted_iota(jnp.int32, (ORDER, ORDER // 2), 0)
    for i, parity in enumerate((core, other)):
        chosen = jnp.where(row_of == wanted + parity * PANEL, 1.0, 0.0).astype(bf16)
        roots_by[i] = dot(roots, chosen).astype(bf16)

    odd_u = [lax.rem(u[h], 2) for h in halves]
    odd_v = [lax.rem(v[h], 2) for h in halves]

    corners = [(a, b) for a in range(2) for b in range(2)]
    for h in halves:
        place = 2 * odd_u[h] + odd_v[h]
        all_of(recv1.at[h], incoming=("step1", h))
        for a, b in corners:
            value = acc[h, a, b]
            for i in range(3):
                value = value + recv1[h, i, a, b].astype(f32)
            shares[h, place, a, b] = value.astype(bf16)
        mine_share = shares.at[h, place]
        for i in range(3):
            send(mine_share, mine_share, small[h][i], "step2", ("step2", h))
    three = recv1.at[0, :, 0, 0]

    def across(ref, name, h):
        block = ref.at[h, u[h], v[h], core]
        for i in range(3):
            send(block, block, small[h][i], "across" + name, ("across" + name, h))

    def group(ref, h, flip_u, flip_v):
        i = 1 - pair_u[h] if flip_u else pair_u[h]
        j = 1 - pair_v[h] if flip_v else pair_v[h]
        return ref.at[h, pl.ds(2 * i, 2), pl.ds(2 * j, 2), core]

    def spread(ref, name, h):
        block = group(ref, h, 0, 0)
        for i in range(3):
            send(block, block, large[h][i], "along" + name, ("along" + name, h, i))

    def hand_over(ref, name, h, flips):
        block = group(ref, h, *flips)
        send(block, block, sibling, "over" + name, "over" + name)

    def collect(ref, name, late):
        for i in (1, 2, 0):
            for h in halves:
                all_of(group(ref, h, *FLIPS[i]), incoming=("along" + name, h, i))
                hand_over(ref, name, h, FLIPS[i])
        late()
        all_of(ref.at[:, :, :, other], incoming="over" + name)

    for h in halves:
        all_of(shares.at[h, 0:3], incoming=("step2", h))
        for a, b in corners:
            value = shares[h, 0, a, b].astype(f32)
            for i in range(1, 4):
                value = value + shares[h, i, a, b].astype(f32)
            total[h, 2 * pair_u[h] + a, 2 * pair_v[h] + b, core] = value.astype(bf16)
        spread(total, "0", h)
    for h in halves:
        hand_over(total, "0", h, (0, 0))

    lane = lax.broadcasted_iota(jnp.int32, (1, 2 * KC), 1)
    is_key = lane < KC

    def to_lanes(square):
        column = jnp.sum(square, axis=0, keepdims=True)
        query = column[:, :128]
        for i in range(1, QC // 128):
            query = query + column[:, 128 * i : 128 * (i + 1)]
        return query, column[:, QC:]

    def my_rows():
        return jnp.concatenate([total[h, u[h], v[h], core] for h in halves], axis=0)

    def graft_part():
        mom_load.wait()
        row_grad = my_rows().astype(f32)
        moment_new = moment_keep * mom_v[...] + moment_add * row_grad * row_grad
        mom_new[...] = moment_new
        graft = row_grad / (jnp.sqrt(moment_new) + graft_eps)
        graft_q, graft_kv = to_lanes(jnp.square(graft))
        norm[0] = jnp.zeros((8, 128), f32)
        norm[0, 0:1, :] = graft_q
        norm[0, 1:2, :] = graft_kv

    def diagonal_part():
        rkvr_load.wait()
        row = lax.broadcasted_iota(jnp.int32, (KC, 2 * KC), 0)
        col = lax.broadcasted_iota(jnp.int32, (KC, 2 * KC), 1)
        for i in range(2):
            place = (col == row + i * KC).astype(f32).astype(bf16)
            diag[KC * i : KC * (i + 1), :] = dot(rkvr_v[i], place).astype(bf16)

    saved = []

    def project(i, parity):
        rows_q = total[:, :, :, parity, :, :QC].reshape(ORDER // 2, QC)
        rows_kv = total[:, :, :, parity, :, QC:].reshape(ORDER // 2, 2 * KC)
        return dot(roots_by[i, :PANEL], rows_q), dot(roots_by[i, PANEL:], rows_kv)

    def wait_loads():
        rqr_load.wait()
        for copy in rest:
            copy.wait()
        saved.append(project(0, core))

    learn(1)
    tell(2)
    graft_part()
    diagonal_part()
    collect(total, "0", wait_loads)

    def query_grad():
        return in_order(total, slice(0, QC))

    def key_value_grad():
        return in_order(total, slice(QC, COLS))

    saved.append(project(1, other))
    proj_q = (saved[0][0] + saved[1][0]).astype(bf16)
    both = saved[0][1] + saved[1][1]
    proj_kv = jnp.where(is_key, both[:PANEL], both[PANEL:]).astype(bf16)
    cond_q = dot(proj_q, rqr_v[...])
    cond_kv = dot(proj_kv, diag[...])

    levels = (
        (0, 8, 4 * lax.rem(x, 2) + 2 * lax.rem(y, 2) + core, large[0] + [sibling] + crossed),
        (8, 4, 2 * odd_u[0] + odd_v[0], large[1]),
        (12, depth, z, on_z),
    )

    def norm_send(level):
        start, _, place, devices = levels[level]
        norm_in[start + place] = norm[level]
        for device in devices:
            send(norm.at[level], norm_in.at[start + place], device, "norm", ("norm", level))

    def norm_add(level):
        start, count, _, _ = levels[level]
        all_of(norm_in.at[start : start + count - 1], incoming=("norm", level))
        value = norm_in[start]
        for i in range(1, count):
            value = value + norm_in[start + i]
        return value

    def norm_step(level):
        norm[level] = norm_add(level - 1)
        norm_send(level)

    square = jnp.square(jnp.concatenate([cond_q, cond_kv], axis=1))
    cond_lanes_q, cond_lanes_kv = to_lanes(square)
    norm[0, 2:3, :] = cond_lanes_q
    norm[0, 3:4, :] = cond_lanes_kv
    norm_send(0)
    for h in halves:
        rows = slice(HALF * h, HALF * (h + 1))
        gathered[h, u[h], v[h], core, :, :QC] = cond_q[rows].astype(bf16)
        gathered[h, u[h], v[h], core, :, QC:] = cond_kv[rows].astype(bf16)
        across(gathered, "1", h)

    def left_part():
        owned = my_rows()
        owned_kv = owned[:, QC:].astype(f32)
        split = jnp.concatenate(
            [jnp.where(is_key, owned_kv, 0.0), jnp.where(is_key, 0.0, owned_kv)], axis=0
        ).astype(bf16)
        both = dot(split, key_value_grad(), 1, 1)
        left_new[1] = factor_keep * lf_v[1] + factor_add * both[:PANEL]
        left_new[2] = factor_keep * lf_v[2] + factor_add * both[PANEL:]
        left_new[0] = factor_keep * lf_v[0] + factor_add * dot(owned[:, :QC], query_grad(), 1, 1)

    def right_part():
        columns = pl.ds(pl.multiple_of(x * 128, 128), 128)
        slab[...] = dot(
            total[..., columns].reshape(ORDER, 128), total[..., :QC].reshape(ORDER, QC), 0, 0
        )
        mine_q = pl.ds(pl.multiple_of(lax.rem(dp, 2 * SIDE) * 16, 16), 16)
        rq_new[...] = factor_keep * rq_v[...] + factor_add * slab[mine_q, :]
        key_value = total[..., QC:].reshape(ORDER, 2 * KC)
        square = dot(key_value, key_value, 0, 0)
        rkv_new[0] = factor_keep * rkv_v[0] + factor_add * square[:KC, :KC]
        moved = pltpu.roll(square, KC, 1)
        rkv_new[1] = factor_keep * rkv_v[1] + factor_add * moved[KC:, :KC]

    left_part()
    norm_step(1)
    for h in halves:
        all_of(three, incoming=("across1", h))
        spread(gathered, "1", h)
    for h in halves:
        hand_over(gathered, "1", h, (0, 0))
    right_part()
    learn(2)
    norm_step(2)

    def scale_part():
        sums = norm_add(2)

        def whole(row_index, mask):
            values = sums[row_index : row_index + 1, :]
            if mask is not None:
                values = jnp.where(mask, values, 0.0)
            return jnp.sum(values, axis=1, keepdims=True)

        def scale(graft_sq, shampoo_sq):
            return jnp.sqrt(graft_sq / (shampoo_sq + norm_eps))

        scale_q = scale(whole(0, None), whole(2, None))
        scale_k = scale(whole(1, is_key), whole(3, is_key))
        scale_v = scale(whole(1, lane >= KC), whole(3, lane >= KC))
        scale_row[:, :QC] = jnp.broadcast_to(scale_q, (8, QC))
        scale_row[:, QC:] = jnp.broadcast_to(jnp.where(is_key, scale_k, scale_v), (8, 2 * KC))

    collect(gathered, "1", scale_part)

    all_of(sib, outgoing="pair")
    all_of(recv1, outgoing="step1")
    all_of(recv1, outgoing="step2")
    all_of(recv1.at[:, :, 0, 0], outgoing="across1")
    for name, ref in (("0", total), ("1", gathered)):
        all_of(recv1, outgoing="along" + name)
        all_of(ref.at[:, :, :, core], outgoing="over" + name)
    all_of(norm_in.at[: 7 + 3 + depth - 1], outgoing="norm")
    assert len(sends) == ssem.shape[0] and len(arrivals) == rsem.shape[0]


def finish(gathered, scale_row, left, rq, rkv, mom, direction, left_out, rq_out, rkv_out, mom_out, rows, sem):
    copies = []

    def store(src, dst):
        copy = pltpu.make_async_copy(src, dst, sem.at[len(copies)])
        copy.start()
        copies.append(copy)

    for src, dst in ((left, left_out), (mom, mom_out), (rq, rq_out), (rkv, rkv_out)):
        store(src, dst)
    height = ORDER // SIDE
    scale = scale_row[0:1, :]
    for i in range(SIDE):
        rows[i] = (in_order(gathered, slice(0, COLS), (i,)).astype(f32) * scale).astype(bf16)
        store(rows.at[i], direction.at[pl.ds(i * height, height)])
    for copy in copies:
        copy.wait()


def local_step(grads, left_factor, left_root, right_q, right_kv, right_q_root, right_kv_root, moment):
    grid = (SIDE, SIDE, 2, 2, HALF, COLS)
    by_half = (2, SIDE, SIDE, 2, HALF, COLS)
    depth = lax.axis_size("mp")
    quad_block = (2, 2, HALF, COLS)
    block = (SIDE, HALF, COLS)
    hbm = pl.BlockSpec(memory_space=pltpu.HBM)
    vmem = pl.BlockSpec(memory_space=pltpu.VMEM)
    shape = jax.ShapeDtypeStruct
    gathered, scale_row, left_new, rq_new, rkv_new, mom_new = pl.pallas_call(
        kernel,
        out_shape=(
            shape(by_half, bf16),
            shape((8, COLS), f32),
            shape((3, PANEL, ORDER), f32),
            shape((16, QC), f32),
            shape((2, KC, KC), f32),
            shape((PANEL, COLS), f32),
        ),
        in_specs=[hbm] * 8,
        out_specs=(vmem,) * 6,
        scratch_shapes=[
            pltpu.VMEM((2, SIDE) + block, bf16),
            pltpu.VMEM((2, SIDE) + block, bf16),
            pltpu.VMEM((2, 3) + quad_block, bf16),
            pltpu.VMEM((2, 3) + quad_block, bf16),
            pltpu.VMEM((2,) + quad_block, f32),
            pltpu.VMEM((2, 4) + quad_block, bf16),
            pltpu.VMEM(by_half, bf16),
            pltpu.VMEM((3, PANEL, ORDER), f32),
            pltpu.VMEM((3, PANEL, ORDER), bf16),
            pltpu.VMEM((16, QC), f32),
            pltpu.VMEM((2, KC, KC), f32),
            pltpu.VMEM((QC, QC), bf16),
            pltpu.VMEM((2, KC, KC), bf16),
            pltpu.VMEM((PANEL, COLS), f32),
            pltpu.VMEM((2, 3 * PANEL, ORDER // 2), bf16),
            pltpu.VMEM((2 * KC, 2 * KC), bf16),
            pltpu.VMEM((128, QC), f32),
            pltpu.VMEM((3, 8, 128), f32),
            pltpu.VMEM((12 + depth, 8, 128), f32),
            pltpu.SemaphoreType.DMA((9,)),
            pltpu.SemaphoreType.DMA((31,)),
            pltpu.SemaphoreType.DMA((15,)),
            pltpu.SemaphoreType.REGULAR((3,)),
        ],
        compiler_params=pltpu.CompilerParams(
            collective_id=0, has_side_effects=True, vmem_limit_bytes=40 * 1024 * 1024
        ),
    )(
        *(
            pltpu.with_memory_space_constraint(array, pltpu.HBM)
            for array in (
                grads.reshape(grid), left_factor[0], left_root[0], right_q[0], right_kv[0],
                right_q_root[0], right_kv_root[0], moment,
            )
        )
    )
    direction, left_new, rq_new, rkv_new, mom_new = pl.pallas_call(
        finish,
        out_shape=(
            shape((ORDER, COLS), bf16),
            shape((3, PANEL, ORDER), f32),
            shape((16, QC), f32),
            shape((2, KC, KC), f32),
            shape((PANEL, COLS), f32),
        ),
        in_specs=[vmem] * 6,
        out_specs=(hbm,) * 5,
        scratch_shapes=[
            pltpu.VMEM((SIDE, ORDER // SIDE, COLS), bf16),
            pltpu.SemaphoreType.DMA((4 + SIDE,)),
        ],
        compiler_params=pltpu.CompilerParams(vmem_limit_bytes=40 * 1024 * 1024),
    )(gathered, scale_row, left_new, rq_new, rkv_new, mom_new)
    return direction, left_new[None], rq_new[None], rkv_new[None], mom_new


def solution(mesh):
    return jax.shard_map(
        local_step,
        mesh=mesh,
        in_specs=(
            P("dp", None, "mp"),
            P("mp", None, "dp", None),
            P("mp", None, "dp", None),
            P("mp", "dp", None),
            P("mp", None, None, None),
            P("mp", None, None),
            P("mp", None, None, None),
            P("dp", "mp"),
        ),
        out_specs=(
            P(None, "mp"),
            P("mp", None, "dp", None),
            P("mp", "dp", None),
            P("mp", None, None, None),
            P("dp", "mp"),
        ),
        check_vma=False,
    )
```

```python
import jax
import jax.numpy as jnp
from jax import lax
from jax.experimental import pallas as pl
from jax.experimental.pallas import tpu as pltpu
from jax.sharding import PartitionSpec as P

MESH = pl.DeviceIdType.MESH
f32 = jnp.float32
bf16 = jnp.bfloat16

factor_keep = 0.95
factor_add = 0.05
moment_keep = 0.99
moment_add = 0.01
graft_eps = 1e-08
norm_eps = 1e-06

SIDE = 4
HALF = 16
QC = 512
KC = 64
COLS = QC + 2 * KC
ORDER = 1024
PANEL = 32
FLIPS = ((1, 1), (1, 0), (0, 1))


def dot(a, b, ca=1, cb=0):
    return lax.dot_general(a, b, (((ca,), (cb,)), ((), ())), preferred_element_type=f32)


def in_order(ref, cols, lines=range(SIDE)):
    return jnp.concatenate(
        [
            ref[h, (i + 1 - h) % SIDE, (j + 1 - h) % SIDE, k, :, cols]
            for i in lines for j in range(SIDE) for k in range(2) for h in range(2)
        ],
        axis=0,
    )


def kernel(
    g, lf, lr, rq, rkv, rqr, rkvr, mom,
    gathered, scale_row, left_new, rq_new, rkv_new, mom_new,
    own, sib, part, recv1, acc, shares, total,
    lf_v, lr_v, rq_v, rkv_v, rqr_v, rkvr_v, mom_v,
    roots_by, diag, slab, norm, norm_in,
    ssem, rsem, lsem, known,
):
    dp = lax.axis_index("dp")
    z = lax.axis_index("mp")
    core = lax.rem(dp, 2)
    other = 1 - core
    y = lax.rem(dp // 2, SIDE)
    x = dp // (2 * SIDE)
    depth = lax.axis_size("mp")

    def at(i, j, k):
        return ((i * SIDE + j) * 2 + k, z)

    sibling = at(x, y, other)
    halves = range(2)
    u = [lax.rem(x + 1, SIDE), x]
    v = [lax.rem(y + 1, SIDE), y]

    def near(place):
        odd = lax.rem(place, 2)
        return place + 1 - 2 * odd, lax.rem(place + SIDE - 1 + 2 * odd, SIDE)

    def back(h, place):
        return lax.rem(place + SIDE - 1 + h, SIDE)

    def quad(h, kind, k):
        i = (x, back(h, near(u[h])[kind]))
        j = (y, back(h, near(v[h])[kind]))
        return [at(i[a], j[b], k) for a, b in FLIPS]

    small = [quad(h, 0, core) for h in halves]
    large = [quad(h, 1, core) for h in halves]
    crossed = quad(0, 1, other)
    far_first = sorted(range(1, depth), key=lambda k: -min(k, depth - k))
    on_z = [(dp, lax.rem(z + k, depth)) for k in far_first]

    def beside(k):
        return [(dp, lax.rem(z + k, depth)), (dp, lax.rem(z + depth - k, depth))]

    barrier = pltpu.get_barrier_semaphore()
    partners = [sibling] + large[0] + large[1] + crossed + beside(1)
    for device in partners:
        pl.semaphore_signal(barrier, inc=1, device_id=device, device_id_type=MESH)

    local = []

    def load(src, dst):
        copy = pltpu.make_async_copy(src, dst, lsem.at[len(local)])
        copy.start()
        local.append(copy)
        return copy

    pair_u = [u[h] // 2 for h in halves]
    pair_v = [v[h] // 2 for h in halves]
    lines = [
        [back(h, 2 * (1 - pair_u[h])), back(h, 3 - 2 * pair_u[h]), back(h, 2 * pair_u[h]), back(h, 2 * pair_u[h] + 1)]
        for h in halves
    ]
    mine = {(h, i): load(g.at[lines[h][i], :, core, h], own.at[h, i]) for i in range(SIDE) for h in halves}
    pl.semaphore_wait(barrier, len(partners))

    def tell(i):
        for device in beside(2**i):
            pl.semaphore_signal(known.at[i], inc=1, device_id=device, device_id_type=MESH)

    def learn(i):
        pl.semaphore_wait(known.at[i], 2)

    tell(0)

    sends = {}
    arrivals = {}

    def send(src, dst, device, outgoing, incoming):
        i = sends.setdefault(outgoing, len(sends))
        j = arrivals.setdefault(incoming, len(arrivals))
        pltpu.make_async_remote_copy(
            src_ref=src, dst_ref=dst, send_sem=ssem.at[i], recv_sem=rsem.at[j],
            device_id=device, device_id_type=MESH,
        ).start()

    def all_of(ref, outgoing=None, incoming=None):
        copy = pltpu.make_async_remote_copy(
            src_ref=ref, dst_ref=ref,
            send_sem=ssem.at[sends[outgoing] if outgoing else 0],
            recv_sem=rsem.at[arrivals[incoming] if incoming else 0],
            device_id=sibling, device_id_type=MESH,
        )
        if outgoing:
            copy.wait_send()
        else:
            copy.wait_recv()

    for i in range(SIDE):
        for h in halves:
            send(g.at[lines[h][i], :, other, h], sib.at[h, i], sibling, "pair", ("pair", h, i))

    mom_load = load(mom, mom_v)
    lr_load = load(lr, lr_v)
    rqr_load = load(rqr, rqr_v)
    rkvr_load = load(rkvr, rkvr_v)
    rest = [load(lf, lf_v), load(rq, rq_v), load(rkv, rkv_v)]

    def pair_sum(h, a, flip_u, flip_v, b):
        i = a if flip_u else 2 + a
        pair = 1 - pair_v[h] if flip_v else pair_v[h]
        j = back(h, 2 * pair + b)
        return own[h, i, j].astype(f32) + sib[h, i, j].astype(f32)

    for flip_u in (1, 0):
        for h in halves:
            for i in (0, 1) if flip_u else (2, 3):
                mine[h, i].wait()
                all_of(sib.at[h, i], incoming=("pair", h, i))
            for flip_v in (1, 0):
                for a in range(2):
                    for b in range(2):
                        value = pair_sum(h, a, flip_u, flip_v, b)
                        if flip_u or flip_v:
                            part[h, FLIPS.index((flip_u, flip_v)), a, b] = value.astype(bf16)
                        else:
                            acc[h, a, b] = value
                if flip_u or flip_v:
                    i = FLIPS.index((flip_u, flip_v))
                    send(part.at[h, i], recv1.at[h, i], large[h][i], "step1", ("step1", h))

    learn(0)
    tell(1)

    lr_load.wait()
    roots = lr_v[...].reshape(3 * PANEL, ORDER)
    column = lax.broadcasted_iota(jnp.int32, (1, ORDER // 2), 1)
    half_of = column >> 8
    u_of = ((column >> 6) + SIDE - 1 + half_of) & (SIDE - 1)
    v_of = ((column >> 4) + SIDE - 1 + half_of) & (SIDE - 1)
    wanted = u_of * 256 + v_of * 64 + half_of * HALF + (column & (HALF - 1))
    row_of = lax.broadcasted_iota(jnp.int32, (ORDER, ORDER // 2), 0)
    for i, parity in enumerate((core, other)):
        chosen = jnp.where(row_of == wanted + parity * PANEL, 1.0, 0.0).astype(bf16)
        roots_by[i] = dot(roots, chosen).astype(bf16)

    odd_u = [lax.rem(u[h], 2) for h in halves]
    odd_v = [lax.rem(v[h], 2) for h in halves]

    corners = [(a, b) for a in range(2) for b in range(2)]
    for h in halves:
        place = 2 * odd_u[h] + odd_v[h]
        all_of(recv1.at[h], incoming=("step1", h))
        for a, b in corners:
            value = acc[h, a, b]
            for i in range(3):
                value = value + recv1[h, i, a, b].astype(f32)
            shares[h, place, a, b] = value.astype(bf16)
        mine_share = shares.at[h, place]
        for i in range(3):
            send(mine_share, mine_share, small[h][i], "step2", ("step2", h))
    three = recv1.at[0, :, 0, 0]

    def across(ref, name, h):
        block = ref.at[h, u[h], v[h], core]
        for i in range(3):
            send(block, block, small[h][i], "across" + name, ("across" + name, h))

    def group(ref, h, flip_u, flip_v):
        i = 1 - pair_u[h] if flip_u else pair_u[h]
        j = 1 - pair_v[h] if flip_v else pair_v[h]
        return ref.at[h, pl.ds(2 * i, 2), pl.ds(2 * j, 2), core]

    def spread(ref, name, h):
        block = group(ref, h, 0, 0)
        for i in range(3):
            send(block, block, large[h][i], "along" + name, ("along" + name, h, i))

    def hand_over(ref, name, h, flips):
        block = group(ref, h, *flips)
        send(block, block, sibling, "over" + name, "over" + name)

    def collect(ref, name, late):
        for i in (1, 2, 0):
            for h in halves:
                all_of(group(ref, h, *FLIPS[i]), incoming=("along" + name, h, i))
                hand_over(ref, name, h, FLIPS[i])
        late()
        all_of(ref.at[:, :, :, other], incoming="over" + name)

    for h in halves:
        all_of(shares.at[h, 0:3], incoming=("step2", h))
        for a, b in corners:
            value = shares[h, 0, a, b].astype(f32)
            for i in range(1, 4):
                value = value + shares[h, i, a, b].astype(f32)
            total[h, 2 * pair_u[h] + a, 2 * pair_v[h] + b, core] = value.astype(bf16)
        spread(total, "0", h)
    for h in halves:
        hand_over(total, "0", h, (0, 0))

    lane = lax.broadcasted_iota(jnp.int32, (1, 2 * KC), 1)
    is_key = lane < KC

    def as_row(square, start):
        column = jnp.sum(square, axis=0, keepdims=True)
        query = column[:, :128]
        for i in range(1, QC // 128):
            query = query + column[:, 128 * i : 128 * (i + 1)]
        tail = column[:, QC:]
        parts = (query, jnp.where(is_key, tail, 0.0), jnp.where(is_key, 0.0, tail))
        row = jnp.zeros((1, 128), f32)
        for i in range(3):
            row = jnp.where(lane == start + i, jnp.sum(parts[i], axis=1, keepdims=True), row)
        return row

    def my_rows():
        return jnp.concatenate([total[h, u[h], v[h], core] for h in halves], axis=0)

    def graft_part():
        mom_load.wait()
        row_grad = my_rows().astype(f32)
        moment_new = moment_keep * mom_v[...] + moment_add * row_grad * row_grad
        mom_new[...] = moment_new
        graft = row_grad / (jnp.sqrt(moment_new) + graft_eps)
        norm[0] = as_row(jnp.square(graft), 0)

    def diagonal_part():
        rkvr_load.wait()
        row = lax.broadcasted_iota(jnp.int32, (KC, 2 * KC), 0)
        col = lax.broadcasted_iota(jnp.int32, (KC, 2 * KC), 1)
        for i in range(2):
            place = (col == row + i * KC).astype(f32).astype(bf16)
            diag[KC * i : KC * (i + 1), :] = dot(rkvr_v[i], place).astype(bf16)

    saved = []

    def project(i, parity):
        rows_q = total[:, :, :, parity, :, :QC].reshape(ORDER // 2, QC)
        rows_kv = total[:, :, :, parity, :, QC:].reshape(ORDER // 2, 2 * KC)
        return dot(roots_by[i, :PANEL], rows_q), dot(roots_by[i, PANEL:], rows_kv)

    def wait_loads():
        rqr_load.wait()
        for copy in rest:
            copy.wait()
        saved.append(project(0, core))

    learn(1)
    tell(2)
    graft_part()
    diagonal_part()
    collect(total, "0", wait_loads)

    def query_grad():
        return in_order(total, slice(0, QC))

    def key_value_grad():
        return in_order(total, slice(QC, COLS))

    saved.append(project(1, other))
    proj_q = (saved[0][0] + saved[1][0]).astype(bf16)
    both = saved[0][1] + saved[1][1]
    proj_kv = jnp.where(is_key, both[:PANEL], both[PANEL:]).astype(bf16)
    cond_q = dot(proj_q, rqr_v[...])
    cond_kv = dot(proj_kv, diag[...])

    levels = (
        (0, 8, 4 * lax.rem(x, 2) + 2 * lax.rem(y, 2) + core, large[0] + [sibling] + crossed),
        (8, 4, 2 * odd_u[0] + odd_v[0], large[1]),
        (12, depth, z, on_z),
    )

    def norm_send(level):
        start, _, place, devices = levels[level]
        norm_in[start + place] = norm[level]
        for device in devices:
            send(norm.at[level], norm_in.at[start + place], device, "norm", ("norm", level))

    def norm_add(level):
        start, count, _, _ = levels[level]
        all_of(norm_in.at[start : start + count - 1], incoming=("norm", level))
        value = norm_in[start]
        for i in range(1, count):
            value = value + norm_in[start + i]
        return value

    def norm_step(level):
        norm[level] = norm_add(level - 1)
        norm_send(level)

    square = jnp.square(jnp.concatenate([cond_q, cond_kv], axis=1))
    norm[0] = norm[0] + as_row(square, 3)
    norm_send(0)
    for h in halves:
        rows = slice(HALF * h, HALF * (h + 1))
        gathered[h, u[h], v[h], core, :, :QC] = cond_q[rows].astype(bf16)
        gathered[h, u[h], v[h], core, :, QC:] = cond_kv[rows].astype(bf16)
        across(gathered, "1", h)

    def left_part():
        owned = my_rows()
        owned_kv = owned[:, QC:].astype(f32)
        split = jnp.concatenate(
            [jnp.where(is_key, owned_kv, 0.0), jnp.where(is_key, 0.0, owned_kv)], axis=0
        ).astype(bf16)
        both = dot(split, key_value_grad(), 1, 1)
        left_new[1] = factor_keep * lf_v[1] + factor_add * both[:PANEL]
        left_new[2] = factor_keep * lf_v[2] + factor_add * both[PANEL:]
        left_new[0] = factor_keep * lf_v[0] + factor_add * dot(owned[:, :QC], query_grad(), 1, 1)

    def right_part():
        columns = pl.ds(pl.multiple_of(x * 128, 128), 128)
        slab[...] = dot(
            total[..., columns].reshape(ORDER, 128), total[..., :QC].reshape(ORDER, QC), 0, 0
        )
        mine_q = pl.ds(pl.multiple_of(lax.rem(dp, 2 * SIDE) * 16, 16), 16)
        rq_new[...] = factor_keep * rq_v[...] + factor_add * slab[mine_q, :]
        key_value = total[..., QC:].reshape(ORDER, 2 * KC)
        square = dot(key_value, key_value, 0, 0)
        rkv_new[0] = factor_keep * rkv_v[0] + factor_add * square[:KC, :KC]
        moved = pltpu.roll(square, KC, 1)
        rkv_new[1] = factor_keep * rkv_v[1] + factor_add * moved[KC:, :KC]

    left_part()
    norm_step(1)
    for h in halves:
        all_of(three, incoming=("across1", h))
        spread(gathered, "1", h)
    learn(2)
    norm_step(2)
    for h in halves:
        hand_over(gathered, "1", h, (0, 0))
    right_part()

    def scale_part():
        sums = norm_add(2)

        scales = jnp.sqrt(sums / (pltpu.roll(sums, 125, 1) + norm_eps))
        scale_q, scale_k, scale_v = (
            jnp.sum(jnp.where(lane == i, scales, 0.0), axis=1, keepdims=True) for i in range(3)
        )
        scale_row[:, :QC] = jnp.broadcast_to(scale_q, (8, QC))
        scale_row[:, QC:] = jnp.broadcast_to(jnp.where(is_key, scale_k, scale_v), (8, 2 * KC))

    collect(gathered, "1", scale_part)

    all_of(sib, outgoing="pair")
    all_of(recv1, outgoing="step1")
    all_of(recv1, outgoing="step2")
    all_of(recv1.at[:, :, 0, 0], outgoing="across1")
    for name, ref in (("0", total), ("1", gathered)):
        all_of(recv1, outgoing="along" + name)
        all_of(ref.at[:, :, :, core], outgoing="over" + name)
    all_of(norm_in.at[: 7 + 3 + depth - 1], outgoing="norm")
    assert len(sends) == ssem.shape[0] and len(arrivals) == rsem.shape[0]


def finish(gathered, scale_row, left, rq, rkv, mom, direction, left_out, rq_out, rkv_out, mom_out, rows, sem):
    copies = []

    def store(src, dst):
        copy = pltpu.make_async_copy(src, dst, sem.at[len(copies)])
        copy.start()
        copies.append(copy)

    for src, dst in ((left, left_out), (mom, mom_out), (rq, rq_out), (rkv, rkv_out)):
        store(src, dst)
    height = ORDER // SIDE
    scale = scale_row[0:1, :]
    for i in range(SIDE):
        rows[i] = (in_order(gathered, slice(0, COLS), (i,)).astype(f32) * scale).astype(bf16)
        store(rows.at[i], direction.at[pl.ds(i * height, height)])
    for copy in copies:
        copy.wait()


def local_step(grads, left_factor, left_root, right_q, right_kv, right_q_root, right_kv_root, moment):
    grid = (SIDE, SIDE, 2, 2, HALF, COLS)
    by_half = (2, SIDE, SIDE, 2, HALF, COLS)
    depth = lax.axis_size("mp")
    quad_block = (2, 2, HALF, COLS)
    block = (SIDE, HALF, COLS)
    hbm = pl.BlockSpec(memory_space=pltpu.HBM)
    vmem = pl.BlockSpec(memory_space=pltpu.VMEM)
    shape = jax.ShapeDtypeStruct
    gathered, scale_row, left_new, rq_new, rkv_new, mom_new = pl.pallas_call(
        kernel,
        out_shape=(
            shape(by_half, bf16),
            shape((8, COLS), f32),
            shape((3, PANEL, ORDER), f32),
            shape((16, QC), f32),
            shape((2, KC, KC), f32),
            shape((PANEL, COLS), f32),
        ),
        in_specs=[hbm] * 8,
        out_specs=(vmem,) * 6,
        scratch_shapes=[
            pltpu.VMEM((2, SIDE) + block, bf16),
            pltpu.VMEM((2, SIDE) + block, bf16),
            pltpu.VMEM((2, 3) + quad_block, bf16),
            pltpu.VMEM((2, 3) + quad_block, bf16),
            pltpu.VMEM((2,) + quad_block, f32),
            pltpu.VMEM((2, 4) + quad_block, bf16),
            pltpu.VMEM(by_half, bf16),
            pltpu.VMEM((3, PANEL, ORDER), f32),
            pltpu.VMEM((3, PANEL, ORDER), bf16),
            pltpu.VMEM((16, QC), f32),
            pltpu.VMEM((2, KC, KC), f32),
            pltpu.VMEM((QC, QC), bf16),
            pltpu.VMEM((2, KC, KC), bf16),
            pltpu.VMEM((PANEL, COLS), f32),
            pltpu.VMEM((2, 3 * PANEL, ORDER // 2), bf16),
            pltpu.VMEM((2 * KC, 2 * KC), bf16),
            pltpu.VMEM((128, QC), f32),
            pltpu.VMEM((3, 1, 128), f32),
            pltpu.VMEM((12 + depth, 1, 128), f32),
            pltpu.SemaphoreType.DMA((9,)),
            pltpu.SemaphoreType.DMA((31,)),
            pltpu.SemaphoreType.DMA((15,)),
            pltpu.SemaphoreType.REGULAR((3,)),
        ],
        compiler_params=pltpu.CompilerParams(
            collective_id=0, has_side_effects=True, vmem_limit_bytes=40 * 1024 * 1024
        ),
    )(
        *(
            pltpu.with_memory_space_constraint(array, pltpu.HBM)
            for array in (
                grads.reshape(grid), left_factor[0], left_root[0], right_q[0], right_kv[0],
                right_q_root[0], right_kv_root[0], moment,
            )
        )
    )
    direction, left_new, rq_new, rkv_new, mom_new = pl.pallas_call(
        finish,
        out_shape=(
            shape((ORDER, COLS), bf16),
            shape((3, PANEL, ORDER), f32),
            shape((16, QC), f32),
            shape((2, KC, KC), f32),
            shape((PANEL, COLS), f32),
        ),
        in_specs=[vmem] * 6,
        out_specs=(hbm,) * 5,
        scratch_shapes=[
            pltpu.VMEM((SIDE, ORDER // SIDE, COLS), bf16),
            pltpu.SemaphoreType.DMA((4 + SIDE,)),
        ],
        compiler_params=pltpu.CompilerParams(vmem_limit_bytes=40 * 1024 * 1024),
    )(gathered, scale_row, left_new, rq_new, rkv_new, mom_new)
    return direction, left_new[None], rq_new[None], rkv_new[None], mom_new


def solution(mesh):
    return jax.shard_map(
        local_step,
        mesh=mesh,
        in_specs=(
            P("dp", None, "mp"),
            P("mp", None, "dp", None),
            P("mp", None, "dp", None),
            P("mp", "dp", None),
            P("mp", None, None, None),
            P("mp", None, None),
            P("mp", None, None, None),
            P("dp", "mp"),
        ),
        out_specs=(
            P(None, "mp"),
            P("mp", None, "dp", None),
            P("mp", "dp", None),
            P("mp", None, None, None),
            P("dp", "mp"),
        ),
        check_vma=False,
    )
```

```python
import jax
import jax.numpy as jnp
from jax import lax
from jax.experimental import pallas as pl
from jax.experimental.pallas import tpu as pltpu
from jax.sharding import PartitionSpec as P

MESH = pl.DeviceIdType.MESH
f32 = jnp.float32
bf16 = jnp.bfloat16

factor_keep = 0.95
factor_add = 0.05
moment_keep = 0.99
moment_add = 0.01
graft_eps = 1e-08
norm_eps = 1e-06

SIDE = 4
HALF = 16
QC = 512
KC = 64
COLS = QC + 2 * KC
ORDER = 1024
PANEL = 32
FLIPS = ((1, 1), (1, 0), (0, 1))


def dot(a, b, ca=1, cb=0):
    return lax.dot_general(a, b, (((ca,), (cb,)), ((), ())), preferred_element_type=f32)


def in_order(ref, cols, lines=range(SIDE)):
    return jnp.concatenate(
        [
            ref[h, (i + 1 - h) % SIDE, (j + 1 - h) % SIDE, k, :, cols]
            for i in lines for j in range(SIDE) for k in range(2) for h in range(2)
        ],
        axis=0,
    )


def kernel(
    g, lf, lr, rq, rkv, rqr, rkvr, mom,
    gathered, scale_row, left_new, rq_new, rkv_new, mom_new,
    own, sib, part, recv1, acc, shares, total,
    lf_v, lr_v, rq_v, rkv_v, rqr_v, rkvr_v, mom_v,
    roots_by, diag, slab, norm, norm_in,
    ssem, rsem, lsem, known,
):
    dp = lax.axis_index("dp")
    z = lax.axis_index("mp")
    core = lax.rem(dp, 2)
    other = 1 - core
    y = lax.rem(dp // 2, SIDE)
    x = dp // (2 * SIDE)
    depth = lax.axis_size("mp")

    def at(i, j, k):
        return ((i * SIDE + j) * 2 + k, z)

    sibling = at(x, y, other)
    halves = range(2)
    u = [lax.rem(x + 1, SIDE), x]
    v = [lax.rem(y + 1, SIDE), y]

    def near(place):
        odd = lax.rem(place, 2)
        return place + 1 - 2 * odd, lax.rem(place + SIDE - 1 + 2 * odd, SIDE)

    def back(h, place):
        return lax.rem(place + SIDE - 1 + h, SIDE)

    def quad(h, kind, k):
        i = (x, back(h, near(u[h])[kind]))
        j = (y, back(h, near(v[h])[kind]))
        return [at(i[a], j[b], k) for a, b in FLIPS]

    small = [quad(h, 0, core) for h in halves]
    large = [quad(h, 1, core) for h in halves]
    crossed = quad(0, 1, other)
    far_first = sorted(range(1, depth), key=lambda k: -min(k, depth - k))
    on_z = [(dp, lax.rem(z + k, depth)) for k in far_first]

    def beside(k):
        return [(dp, lax.rem(z + k, depth)), (dp, lax.rem(z + depth - k, depth))]

    barrier = pltpu.get_barrier_semaphore()
    partners = [sibling] + large[0] + large[1] + crossed + beside(1)
    for device in partners:
        pl.semaphore_signal(barrier, inc=1, device_id=device, device_id_type=MESH)

    local = []

    def load(src, dst):
        copy = pltpu.make_async_copy(src, dst, lsem.at[len(local)])
        copy.start()
        local.append(copy)
        return copy

    pair_u = [u[h] // 2 for h in halves]
    pair_v = [v[h] // 2 for h in halves]
    lines = [
        [back(h, 2 * (1 - pair_u[h])), back(h, 3 - 2 * pair_u[h]), back(h, 2 * pair_u[h]), back(h, 2 * pair_u[h] + 1)]
        for h in halves
    ]
    mine = {(h, i): load(g.at[lines[h][i], :, core, h], own.at[h, i]) for i in range(SIDE) for h in halves}
    pl.semaphore_wait(barrier, len(partners))

    def tell(i):
        for device in beside(2**i):
            pl.semaphore_signal(known.at[i], inc=1, device_id=device, device_id_type=MESH)

    def learn(i):
        pl.semaphore_wait(known.at[i], 2)

    tell(0)

    sends = {}
    arrivals = {}

    def send(src, dst, device, outgoing, incoming):
        i = sends.setdefault(outgoing, len(sends))
        j = arrivals.setdefault(incoming, len(arrivals))
        pltpu.make_async_remote_copy(
            src_ref=src, dst_ref=dst, send_sem=ssem.at[i], recv_sem=rsem.at[j],
            device_id=device, device_id_type=MESH,
        ).start()

    def all_of(ref, outgoing=None, incoming=None):
        copy = pltpu.make_async_remote_copy(
            src_ref=ref, dst_ref=ref,
            send_sem=ssem.at[sends[outgoing] if outgoing else 0],
            recv_sem=rsem.at[arrivals[incoming] if incoming else 0],
            device_id=sibling, device_id_type=MESH,
        )
        if outgoing:
            copy.wait_send()
        else:
            copy.wait_recv()

    for i in range(SIDE):
        for h in halves:
            send(g.at[lines[h][i], :, other, h], sib.at[h, i], sibling, "pair", ("pair", h, i))

    mom_load = load(mom, mom_v)
    lr_load = load(lr, lr_v)
    rqr_load = load(rqr, rqr_v)
    rkvr_load = load(rkvr, rkvr_v)
    rest = [load(lf, lf_v), load(rq, rq_v), load(rkv, rkv_v)]

    def pair_sum(h, a, flip_u, flip_v, b):
        i = a if flip_u else 2 + a
        pair = 1 - pair_v[h] if flip_v else pair_v[h]
        j = back(h, 2 * pair + b)
        return own[h, i, j].astype(f32) + sib[h, i, j].astype(f32)

    for flip_u in (1, 0):
        for h in halves:
            for i in (0, 1) if flip_u else (2, 3):
                mine[h, i].wait()
                all_of(sib.at[h, i], incoming=("pair", h, i))
            for flip_v in (1, 0):
                for a in range(2):
                    for b in range(2):
                        value = pair_sum(h, a, flip_u, flip_v, b)
                        if flip_u or flip_v:
                            part[h, FLIPS.index((flip_u, flip_v)), a, b] = value.astype(bf16)
                        else:
                            acc[h, a, b] = value
                if flip_u or flip_v:
                    i = FLIPS.index((flip_u, flip_v))
                    send(part.at[h, i], recv1.at[h, i], large[h][i], "step1", ("step1", h))

    learn(0)
    tell(1)

    lr_load.wait()
    roots = lr_v[...].reshape(3 * PANEL, ORDER)
    column = lax.broadcasted_iota(jnp.int32, (1, ORDER // 2), 1)
    half_of = column >> 8
    u_of = ((column >> 6) + SIDE - 1 + half_of) & (SIDE - 1)
    v_of = ((column >> 4) + SIDE - 1 + half_of) & (SIDE - 1)
    wanted = u_of * 256 + v_of * 64 + half_of * HALF + (column & (HALF - 1))
    row_of = lax.broadcasted_iota(jnp.int32, (ORDER, ORDER // 2), 0)
    for i, parity in enumerate((core, other)):
        chosen = jnp.where(row_of == wanted + parity * PANEL, 1.0, 0.0).astype(bf16)
        roots_by[i] = dot(roots, chosen).astype(bf16)

    odd_u = [lax.rem(u[h], 2) for h in halves]
    odd_v = [lax.rem(v[h], 2) for h in halves]

    corners = [(a, b) for a in range(2) for b in range(2)]
    for h in halves:
        place = 2 * odd_u[h] + odd_v[h]
        all_of(recv1.at[h], incoming=("step1", h))
        for a, b in corners:
            value = acc[h, a, b]
            for i in range(3):
                value = value + recv1[h, i, a, b].astype(f32)
            shares[h, place, a, b] = value.astype(bf16)
        mine_share = shares.at[h, place]
        for i in range(3):
            send(mine_share, mine_share, small[h][i], "step2", ("step2", h))
    three = recv1.at[0, :, 0, 0]

    def across(ref, name, h):
        block = ref.at[h, u[h], v[h], core]
        for i in range(3):
            send(block, block, small[h][i], "across" + name, ("across" + name, h))

    def group(ref, h, flip_u, flip_v):
        i = 1 - pair_u[h] if flip_u else pair_u[h]
        j = 1 - pair_v[h] if flip_v else pair_v[h]
        return ref.at[h, pl.ds(2 * i, 2), pl.ds(2 * j, 2), core]

    def spread(ref, name, h):
        block = group(ref, h, 0, 0)
        for i in range(3):
            send(block, block, large[h][i], "along" + name, ("along" + name, h, i))

    def hand_over(ref, name, h, flips):
        block = group(ref, h, *flips)
        send(block, block, sibling, "over" + name, "over" + name)

    def collect(ref, name, late):
        for i in (1, 2, 0):
            for h in halves:
                all_of(group(ref, h, *FLIPS[i]), incoming=("along" + name, h, i))
                hand_over(ref, name, h, FLIPS[i])
        late()
        all_of(ref.at[:, :, :, other], incoming="over" + name)

    for h in halves:
        all_of(shares.at[h, 0:3], incoming=("step2", h))
        for a, b in corners:
            value = shares[h, 0, a, b].astype(f32)
            for i in range(1, 4):
                value = value + shares[h, i, a, b].astype(f32)
            total[h, 2 * pair_u[h] + a, 2 * pair_v[h] + b, core] = value.astype(bf16)
        spread(total, "0", h)
    for h in halves:
        hand_over(total, "0", h, (0, 0))

    lane = lax.broadcasted_iota(jnp.int32, (1, 2 * KC), 1)
    is_key = lane < KC

    def as_row(square, start):
        column = jnp.sum(square, axis=0, keepdims=True)
        query = column[:, :128]
        for i in range(1, QC // 128):
            query = query + column[:, 128 * i : 128 * (i + 1)]
        tail = column[:, QC:]
        parts = (query, jnp.where(is_key, tail, 0.0), jnp.where(is_key, 0.0, tail))
        row = jnp.zeros((1, 128), f32)
        for i in range(3):
            row = jnp.where(lane == start + i, jnp.sum(parts[i], axis=1, keepdims=True), row)
        return row

    def my_rows():
        return jnp.concatenate([total[h, u[h], v[h], core] for h in halves], axis=0)

    def graft_part():
        mom_load.wait()
        row_grad = my_rows().astype(f32)
        moment_new = moment_keep * mom_v[...] + moment_add * row_grad * row_grad
        mom_new[...] = moment_new
        graft = row_grad / (jnp.sqrt(moment_new) + graft_eps)
        norm[0] = as_row(jnp.square(graft), 0)

    def diagonal_part():
        rkvr_load.wait()
        row = lax.broadcasted_iota(jnp.int32, (KC, 2 * KC), 0)
        col = lax.broadcasted_iota(jnp.int32, (KC, 2 * KC), 1)
        for i in range(2):
            place = (col == row + i * KC).astype(f32).astype(bf16)
            diag[KC * i : KC * (i + 1), :] = dot(rkvr_v[i], place).astype(bf16)

    saved = []

    def project(i, parity):
        rows_q = total[:, :, :, parity, :, :QC].reshape(ORDER // 2, QC)
        rows_kv = total[:, :, :, parity, :, QC:].reshape(ORDER // 2, 2 * KC)
        return dot(roots_by[i, :PANEL], rows_q), dot(roots_by[i, PANEL:], rows_kv)

    def wait_loads():
        rqr_load.wait()
        for copy in rest:
            copy.wait()
        saved.append(project(0, core))

    learn(1)
    tell(2)
    graft_part()
    diagonal_part()
    collect(total, "0", wait_loads)

    def query_grad():
        return in_order(total, slice(0, QC))

    def key_value_grad():
        return in_order(total, slice(QC, COLS))

    saved.append(project(1, other))
    proj_q = (saved[0][0] + saved[1][0]).astype(bf16)
    both = saved[0][1] + saved[1][1]
    proj_kv = jnp.where(is_key, both[:PANEL], both[PANEL:]).astype(bf16)
    cond_q = dot(proj_q, rqr_v[...])
    cond_kv = dot(proj_kv, diag[...])

    levels = (
        (0, 8, 4 * lax.rem(x, 2) + 2 * lax.rem(y, 2) + core, large[0] + [sibling] + crossed),
        (8, 4, 2 * odd_u[0] + odd_v[0], large[1]),
        (12, depth, z, on_z),
    )

    def norm_send(level):
        start, _, place, devices = levels[level]
        norm_in[start + place] = norm[level]
        for device in devices:
            send(norm.at[level], norm_in.at[start + place], device, "norm", ("norm", level))

    def norm_add(level):
        start, count, _, _ = levels[level]
        all_of(norm_in.at[start : start + count - 1], incoming=("norm", level))
        value = norm_in[start]
        for i in range(1, count):
            value = value + norm_in[start + i]
        return value

    def norm_step(level):
        norm[level] = norm_add(level - 1)
        norm_send(level)

    square = jnp.square(jnp.concatenate([cond_q, cond_kv], axis=1))
    norm[0] = norm[0] + as_row(square, 3)
    norm_send(0)
    for h in halves:
        rows = slice(HALF * h, HALF * (h + 1))
        gathered[h, u[h], v[h], core, :, :QC] = cond_q[rows].astype(bf16)
        gathered[h, u[h], v[h], core, :, QC:] = cond_kv[rows].astype(bf16)
        across(gathered, "1", h)

    def left_part():
        owned = my_rows()
        owned_kv = owned[:, QC:].astype(f32)
        split = jnp.concatenate(
            [jnp.where(is_key, owned_kv, 0.0), jnp.where(is_key, 0.0, owned_kv)], axis=0
        ).astype(bf16)
        both = dot(split, key_value_grad(), 1, 1)
        left_new[1] = factor_keep * lf_v[1] + factor_add * both[:PANEL]
        left_new[2] = factor_keep * lf_v[2] + factor_add * both[PANEL:]
        left_new[0] = factor_keep * lf_v[0] + factor_add * dot(owned[:, :QC], query_grad(), 1, 1)

    def right_part():
        columns = pl.ds(pl.multiple_of(x * 128, 128), 128)
        slab[...] = dot(
            total[..., columns].reshape(ORDER, 128), total[..., :QC].reshape(ORDER, QC), 0, 0
        )
        mine_q = pl.ds(pl.multiple_of(lax.rem(dp, 2 * SIDE) * 16, 16), 16)
        rq_new[...] = factor_keep * rq_v[...] + factor_add * slab[mine_q, :]
        key_value = total[..., QC:].reshape(ORDER, 2 * KC)
        square = dot(key_value, key_value, 0, 0)
        rkv_new[0] = factor_keep * rkv_v[0] + factor_add * square[:KC, :KC]
        moved = pltpu.roll(square, KC, 1)
        rkv_new[1] = factor_keep * rkv_v[1] + factor_add * moved[KC:, :KC]

    for h in halves:
        all_of(three, incoming=("across1", h))
        spread(gathered, "1", h)
    norm_step(1)
    left_part()
    learn(2)
    norm_step(2)
    for h in halves:
        hand_over(gathered, "1", h, (0, 0))
    right_part()

    def scale_part():
        sums = norm_add(2)

        scales = jnp.sqrt(sums / (pltpu.roll(sums, 125, 1) + norm_eps))
        scale_q, scale_k, scale_v = (
            jnp.sum(jnp.where(lane == i, scales, 0.0), axis=1, keepdims=True) for i in range(3)
        )
        scale_row[:, :QC] = jnp.broadcast_to(scale_q, (8, QC))
        scale_row[:, QC:] = jnp.broadcast_to(jnp.where(is_key, scale_k, scale_v), (8, 2 * KC))

    collect(gathered, "1", scale_part)

    all_of(sib, outgoing="pair")
    all_of(recv1, outgoing="step1")
    all_of(recv1, outgoing="step2")
    all_of(recv1.at[:, :, 0, 0], outgoing="across1")
    for name, ref in (("0", total), ("1", gathered)):
        all_of(recv1, outgoing="along" + name)
        all_of(ref.at[:, :, :, core], outgoing="over" + name)
    all_of(norm_in.at[: 7 + 3 + depth - 1], outgoing="norm")
    assert len(sends) == ssem.shape[0] and len(arrivals) == rsem.shape[0]


def finish(gathered, scale_row, left, rq, rkv, mom, direction, left_out, rq_out, rkv_out, mom_out, rows, sem):
    copies = []

    def store(src, dst):
        copy = pltpu.make_async_copy(src, dst, sem.at[len(copies)])
        copy.start()
        copies.append(copy)

    for src, dst in ((left, left_out), (mom, mom_out), (rq, rq_out), (rkv, rkv_out)):
        store(src, dst)
    height = ORDER // SIDE
    scale = scale_row[0:1, :]
    for i in range(SIDE):
        rows[i] = (in_order(gathered, slice(0, COLS), (i,)).astype(f32) * scale).astype(bf16)
        store(rows.at[i], direction.at[pl.ds(i * height, height)])
    for copy in copies:
        copy.wait()


def local_step(grads, left_factor, left_root, right_q, right_kv, right_q_root, right_kv_root, moment):
    grid = (SIDE, SIDE, 2, 2, HALF, COLS)
    by_half = (2, SIDE, SIDE, 2, HALF, COLS)
    depth = lax.axis_size("mp")
    quad_block = (2, 2, HALF, COLS)
    block = (SIDE, HALF, COLS)
    hbm = pl.BlockSpec(memory_space=pltpu.HBM)
    vmem = pl.BlockSpec(memory_space=pltpu.VMEM)
    shape = jax.ShapeDtypeStruct
    gathered, scale_row, left_new, rq_new, rkv_new, mom_new = pl.pallas_call(
        kernel,
        out_shape=(
            shape(by_half, bf16),
            shape((8, COLS), f32),
            shape((3, PANEL, ORDER), f32),
            shape((16, QC), f32),
            shape((2, KC, KC), f32),
            shape((PANEL, COLS), f32),
        ),
        in_specs=[hbm] * 8,
        out_specs=(vmem,) * 6,
        scratch_shapes=[
            pltpu.VMEM((2, SIDE) + block, bf16),
            pltpu.VMEM((2, SIDE) + block, bf16),
            pltpu.VMEM((2, 3) + quad_block, bf16),
            pltpu.VMEM((2, 3) + quad_block, bf16),
            pltpu.VMEM((2,) + quad_block, f32),
            pltpu.VMEM((2, 4) + quad_block, bf16),
            pltpu.VMEM(by_half, bf16),
            pltpu.VMEM((3, PANEL, ORDER), f32),
            pltpu.VMEM((3, PANEL, ORDER), bf16),
            pltpu.VMEM((16, QC), f32),
            pltpu.VMEM((2, KC, KC), f32),
            pltpu.VMEM((QC, QC), bf16),
            pltpu.VMEM((2, KC, KC), bf16),
            pltpu.VMEM((PANEL, COLS), f32),
            pltpu.VMEM((2, 3 * PANEL, ORDER // 2), bf16),
            pltpu.VMEM((2 * KC, 2 * KC), bf16),
            pltpu.VMEM((128, QC), f32),
            pltpu.VMEM((3, 1, 128), f32),
            pltpu.VMEM((12 + depth, 1, 128), f32),
            pltpu.SemaphoreType.DMA((9,)),
            pltpu.SemaphoreType.DMA((31,)),
            pltpu.SemaphoreType.DMA((15,)),
            pltpu.SemaphoreType.REGULAR((3,)),
        ],
        compiler_params=pltpu.CompilerParams(
            collective_id=0, has_side_effects=True, vmem_limit_bytes=40 * 1024 * 1024
        ),
    )(
        *(
            pltpu.with_memory_space_constraint(array, pltpu.HBM)
            for array in (
                grads.reshape(grid), left_factor[0], left_root[0], right_q[0], right_kv[0],
                right_q_root[0], right_kv_root[0], moment,
            )
        )
    )
    direction, left_new, rq_new, rkv_new, mom_new = pl.pallas_call(
        finish,
        out_shape=(
            shape((ORDER, COLS), bf16),
            shape((3, PANEL, ORDER), f32),
            shape((16, QC), f32),
            shape((2, KC, KC), f32),
            shape((PANEL, COLS), f32),
        ),
        in_specs=[vmem] * 6,
        out_specs=(hbm,) * 5,
        scratch_shapes=[
            pltpu.VMEM((SIDE, ORDER // SIDE, COLS), bf16),
            pltpu.SemaphoreType.DMA((4 + SIDE,)),
        ],
        compiler_params=pltpu.CompilerParams(vmem_limit_bytes=40 * 1024 * 1024),
    )(gathered, scale_row, left_new, rq_new, rkv_new, mom_new)
    return direction, left_new[None], rq_new[None], rkv_new[None], mom_new


def solution(mesh):
    return jax.shard_map(
        local_step,
        mesh=mesh,
        in_specs=(
            P("dp", None, "mp"),
            P("mp", None, "dp", None),
            P("mp", None, "dp", None),
            P("mp", "dp", None),
            P("mp", None, None, None),
            P("mp", None, None),
            P("mp", None, None, None),
            P("dp", "mp"),
        ),
        out_specs=(
            P(None, "mp"),
            P("mp", None, "dp", None),
            P("mp", "dp", None),
            P("mp", None, None, None),
            P("dp", "mp"),
        ),
        check_vma=False,
    )
```
